256 devices in a mesh: ctx: 16 (over x, y_hi, core), ch: 16 (over z, y_lo).
Axes of the slice: x: 4, y: 4 (y_hi: 2, y_lo: 2; y = y_hi * 2 + y_lo), z: 8, core: 2. Of those that a mesh axis runs over, the one named last changes fastest.
Arguments:
- out_gate: bfloat16 [2048, 8192], P('ctx', 'ch'), may hold values from -6 to 6
- in_gate: bfloat16 [2048, 8192], P('ctx', 'ch'), may hold values from -6 to 6
- values: bfloat16 [2048, 8192], P('ctx', 'ch'), may hold values from -6 to 6
- filter_taps: bfloat16 [2048, 8192], P(None, 'ch'), may hold values from -1.1 to 1.1, as said below
- upstream: bfloat16 [2048, 8192], P('ctx', 'ch'), may hold values from -6 to 6
Outputs:
- mixed_out: bfloat16 [2048, 8192], P('ctx', 'ch')
- grad_out_gate: bfloat16 [2048, 8192], P('ctx', 'ch')
- grad_in_gate: bfloat16 [2048, 8192], P('ctx', 'ch')
- grad_values: bfloat16 [2048, 8192], P('ctx', 'ch')
- grad_filter: float32 [2048, 8192], P(('ctx', 'ch'))
The draws below stay inside these ranges and needn't reach their ends.
Inputs may be any that keep to these rules, and one draw needn't show every extreme that they name: `filter_taps`: taps of the causal filter, lag first.
All inputs are finite; a program needn't handle non-finite values.
Results may differ from the reference program's by a relative error of at most 0.0049.
Values may be sent and summed in bfloat16 or wider, within the bound.
No kernel may reach another device: no remote copies, remote signals or barrier semaphores. Data moves between devices by JAX's collectives and lax.ppermute only.
A program may use at most 64 MiB of HBM per device.

```python
import jax
import jax.numpy as jnp
from jax import lax

D = 8192
SEQ = 2048


def draw_filter_taps(key, part):
    key = jax.random.fold_in(key, 11)
    key_rate, key_taps = jax.random.split(key)
    lags = jnp.arange(SEQ, dtype=jnp.float32)[:, None]
    spans = jnp.exp(jax.random.uniform(key_rate, (1, D), jnp.float32, jnp.log(30.0), jnp.log(16.0 * SEQ)))
    rough = jax.random.truncated_normal(key_taps, -4.0, 4.0, (SEQ, D), jnp.float32)
    amplitude = jnp.sqrt(2.0 / jnp.minimum(spans, 1.0 * SEQ))
    return (amplitude * jnp.exp(-lags / spans) * rough).astype(jnp.bfloat16)


def block_scale(stream_key, dims, cuts, smallest, high):
    level, own = 1.0, jax.random.fold_in(stream_key, 6)
    for axis_at, parts in cuts:
        steps = jnp.exp(jax.random.uniform(jax.random.fold_in(own, axis_at), (parts,), jnp.float32, smallest / len(cuts), high / len(cuts)))
        level = level * jnp.repeat(steps, dims[axis_at] // parts).reshape([-1 if axis == axis_at else 1 for axis in range(len(dims))])
    return level


def bell_draw(stream_key, dims, scale, limit, cuts=(), kind=jnp.bfloat16):
    level = block_scale(stream_key, dims, cuts, -0.22, 0.18) if cuts else 1.0
    values = jax.random.normal(stream_key, dims, jnp.float32) * scale * level
    return jnp.minimum(jnp.maximum(values, -limit), limit).astype(kind)


def setup_inputs(seed: int = 0) -> dict:
    streams_of = jax.random.split(jax.random.key(seed), 6)
    return {
        "out_gate": bell_draw(streams_of[0], (SEQ, D), 1.0, 6.0, ((0, 16), (1, 16))),
        "in_gate": bell_draw(streams_of[1], (SEQ, D), 1.0, 6.0, ((0, 16), (1, 16))),
        "values": bell_draw(streams_of[2], (SEQ, D), 1.0, 6.0, ((0, 16), (1, 16))),
        "filter_taps": draw_filter_taps(jax.random.fold_in(streams_of[5], 71), 0),
        "upstream": bell_draw(streams_of[4], (SEQ, D), 1.0, 6.0, ((0, 16), (1, 16))),
    }


def causal(signal, kernel):
    length = signal.shape[0]
    spectrum = jnp.fft.rfft(signal, 2 * length, axis=0) * jnp.fft.rfft(kernel, 2 * length, axis=0)
    return jnp.fft.irfft(spectrum, 2 * length, axis=0)[:length]


def reference(out_gate, in_gate, values, filter_taps, upstream):
    product = (in_gate.astype(jnp.float32) * values.astype(jnp.float32)).astype(jnp.bfloat16)
    cotangent = (upstream.astype(jnp.float32) * out_gate.astype(jnp.float32)).astype(jnp.bfloat16)
    mixed_rows = lax.optimization_barrier(product).astype(jnp.float32)
    grad_rows = lax.optimization_barrier(cotangent).astype(jnp.float32)
    taps_wide = filter_taps.astype(jnp.float32)
    filtered = causal(mixed_rows, taps_wide)
    mixed_out = (out_gate.astype(jnp.float32) * filtered).astype(jnp.bfloat16)
    grad_out_gate = (upstream.astype(jnp.float32) * filtered).astype(jnp.bfloat16)
    flipped = grad_rows[::-1]
    grad_mixed = causal(flipped, taps_wide)[::-1]
    grad_in_gate = (grad_mixed * values.astype(jnp.float32)).astype(jnp.bfloat16)
    grad_values = (grad_mixed * in_gate.astype(jnp.float32)).astype(jnp.bfloat16)
    grad_filter = causal(flipped, mixed_rows)[::-1] * (SEQ ** -0.5)
    return mixed_out, grad_out_gate, grad_in_gate, grad_values, grad_filter
```

```python
import math

import jax
import jax.numpy as jnp
import ml_dtypes
import numpy as np
from jax import lax
from jax.experimental import pallas as pl
from jax.experimental.pallas import tpu as pltpu
from jax.sharding import PartitionSpec as P

VMEM = 48 * 1024 * 1024
f32, bf16 = jnp.float32, jnp.bfloat16


def leaf_angles(count, theta):
    if count == 1:
        return [theta]
    return leaf_angles(count // 2, theta / 2) + leaf_angles(count // 2, theta / 2 + math.pi)


def evaluate(coefs, theta):
    if len(coefs) == 1:
        return coefs
    half = len(coefs) // 2
    wr, wi = math.cos(theta / 2), math.sin(theta / 2)
    plus, minus = [], []
    for (lr, li), (hr, hi) in zip(coefs[:half], coefs[half:]):
        if hi is None:
            tr, ti = hr * wr, hr * wi
            plus.append((lr + tr, ti))
            minus.append((lr - tr, -ti))
        else:
            tr, ti = hr * wr - hi * wi, hr * wi + hi * wr
            plus.append((lr + tr, li + ti))
            minus.append((lr - tr, li - ti))
    return evaluate(plus, theta / 2) + evaluate(minus, theta / 2 + math.pi)


def interpolate(values, theta, real):
    if len(values) == 1:
        return values
    half = len(values) // 2
    wr, wi = math.cos(theta / 2), math.sin(theta / 2)
    plus = interpolate(values[:half], theta / 2, False)
    minus = interpolate(values[half:], theta / 2 + math.pi, False)
    low, high = [], []
    for (pr, pi), (mr, mi) in zip(plus, minus):
        dr, di = pr - mr, pi - mi
        if real:
            low.append(pr + mr)
            high.append(dr * wr + di * wi)
        else:
            low.append((pr + mr, pi + mi))
            high.append((dr * wr + di * wi, di * wr - dr * wi))
    return low + high


def tables(blocks, outer):
    phi = np.array(leaf_angles(blocks, math.pi / 2))
    b = np.arange(outer)
    twist = np.exp(1j * phi[:, None] * b[None, :] / outer)
    twist = np.concatenate([twist.real, twist.imag], 0).astype(np.float32)
    w = np.exp(2j * np.pi * (np.outer(b, b) % outer) / outer)
    forward = np.block([[w.real, w.imag], [-w.imag, w.real]])
    v = np.conj(w) / (blocks * outer)
    backward = np.block([[v.real, v.imag], [-v.imag, v.real]])

    def split(m):
        top = m.astype(np.float32).astype(ml_dtypes.bfloat16)
        rest = (m - top.astype(np.float64)).astype(np.float32).astype(ml_dtypes.bfloat16)
        return np.stack([top, rest])

    return twist, split(forward), split(backward)


def accurate_dot(x, m_ref):
    top = x.astype(bf16)
    rest = (x - top.astype(f32)).astype(bf16)
    dot = lambda a, b: jnp.dot(a, b, preferred_element_type=f32)
    return dot(top, m_ref[0]) + (dot(rest, m_ref[0]) + dot(top, m_ref[1]))


def send_kernel(out_gate, in_gate, values, upstream, send):
    blocks, width = send.shape[0], send.shape[1] // 2
    product = (in_gate[...].astype(f32) * values[...].astype(f32)).astype(bf16)
    cotangent = (upstream[...].astype(f32) * out_gate[...].astype(f32)).astype(bf16)
    rows = product.shape[0]
    send[:, :width, :] = product.T.reshape(blocks, width, rows)
    send[:, width:, :] = cotangent.T.reshape(blocks, width, rows)


def forward_part(load, twist, matrix, work, width, outer):
    blocks = twist.shape[0] // 2
    for g in range(width // 16):
        coefs = [(load(i, g), None) for i in range(blocks)]
        for k, (re, im) in enumerate(evaluate(coefs, math.pi / 2)):
            cr, ci = twist[k : k + 1, :], twist[blocks + k : blocks + k + 1, :]
            at = slice(k * width + 16 * g, k * width + 16 * g + 16)
            work[at, :outer] = re * cr - im * ci
            work[at, outer:] = re * ci + im * cr
    step = 128
    for r in range(0, blocks * width, step):
        work[r : r + step, :] = accurate_dot(work[r : r + step, :], matrix)


def taps_kernel(index, taps, twist, matrix, spectrum, turned):
    blocks, outer = twist.shape[0] // 2, twist.shape[1]
    width = spectrum.shape[0] // blocks
    for i in range(blocks):
        turned[i] = taps[i * outer : (i + 1) * outer, :].astype(f32).T
    start = pl.multiple_of(index[1], 16)

    def load(i, g):
        return turned[i, pl.ds(start + 16 * g, 16), :]

    forward_part(load, twist, matrix, spectrum, width, outer)


def mix_kernel(received, taps_values, twist, forward, backward, result, work):
    blocks, width, outer = received.shape[0], received.shape[1] // 2, received.shape[2]
    for s in range(2):
        forward_part(
            lambda i, g: received[i, s * width + 16 * g : s * width + 16 * g + 16, :].astype(f32),
            twist, forward, work.at[s], width, outer,
        )
    step = 128
    for r in range(0, blocks * width, step):
        at = slice(r, r + step)
        pr, pi = work[0, at, :outer], work[0, at, outer:]
        cr, ci = work[1, at, :outer], work[1, at, outer:]
        hr, hi = taps_values[at, :outer], taps_values[at, outer:]
        filtered = jnp.concatenate([hr * pr - hi * pi, hr * pi + hi * pr], 1)
        mixed = jnp.concatenate([cr * hr + ci * hi, ci * hr - cr * hi], 1)
        lags = jnp.concatenate([cr * pr + ci * pi, ci * pr - cr * pi], 1)
        work[0, at, :] = accurate_dot(filtered, backward)
        work[1, at, :] = accurate_dot(mixed, backward)
        work[2, at, :] = accurate_dot(lags, backward)
    norm_factor = (blocks * outer) ** -0.5
    for s in range(3):
        for g in range(width // 16):
            values = []
            for k in range(blocks):
                cr, ci = twist[k : k + 1, :], twist[blocks + k : blocks + k + 1, :]
                at = slice(k * width + 16 * g, k * width + 16 * g + 16)
                re, im = work[s, at, :outer], work[s, at, outer:]
                values.append((re * cr + im * ci, im * cr - re * ci))
            for i, x in enumerate(interpolate(values, math.pi / 2, True)):
                if s == 2:
                    x = x * norm_factor
                result[i, s * width + 16 * g : s * width + 16 * g + 16, :] = x.astype(bf16)


def lags_kernel(back, lags):
    width = back.shape[1] // 3
    part = back[:, 2 * width :, :].astype(f32)
    turned = part.reshape(part.shape[0] * width, part.shape[2]).T
    lags[...] = turned.reshape(lags.shape)


def gates_kernel(back, out_gate, in_gate, values, upstream, mixed_out, d_out_gate, d_in_gate, d_values):
    width = back.shape[1] // 3
    rows = back.shape[2]

    def part(s):
        x = back[:, s * width : (s + 1) * width, :].astype(f32)
        return x.reshape(x.shape[0] * width, rows).T

    filtered, grad_mixed = part(0), part(1)
    mixed_out[...] = (out_gate[...].astype(f32) * filtered).astype(bf16)
    d_out_gate[...] = (upstream[...].astype(f32) * filtered).astype(bf16)
    d_in_gate[...] = (grad_mixed * values[...].astype(f32)).astype(bf16)
    d_values[...] = (grad_mixed * in_gate[...].astype(f32)).astype(bf16)


def join_kernel(arrived, grad_filter):
    span = arrived.shape[2]
    for j in range(arrived.shape[0]):
        grad_filter[:, j * span : (j + 1) * span] = arrived[j].astype(f32)


def call(kernel, outs, *args, flops=1000000, **kwargs):
    return pl.pallas_call(
        kernel,
        out_shape=outs,
        compiler_params=pltpu.CompilerParams(vmem_limit_bytes=VMEM),
        cost_estimate=pl.CostEstimate(flops=flops, bytes_accessed=1 << 20, transcendentals=0),
        **kwargs,
    )(*args)


def body(out_gate, in_gate, values, filter_taps, upstream):
    rows, channels = out_gate.shape
    seq_len = filter_taps.shape[0]
    blocks = lax.axis_size("ctx")
    owners = lax.axis_size("ch")
    width = channels // blocks
    shape = jax.ShapeDtypeStruct
    twist, forward, backward = (jnp.asarray(t) for t in tables(blocks, rows))

    send = call(send_kernel, shape((blocks, 2 * width, rows), bf16), out_gate, in_gate, values, upstream)
    received = lax.all_to_all(send, "ctx", 0, 0, tiled=True)

    me = lax.axis_index("ctx")
    first = me * width
    index = jnp.stack([first // 128, first % 128]).astype(jnp.int32)
    whole = lambda s: pl.BlockSpec(s, lambda g, index: (0,) * len(s))
    taps_values = call(
        taps_kernel,
        shape((blocks * width, 2 * rows), f32),
        index, filter_taps, twist, forward,
        grid_spec=pltpu.PrefetchScalarGridSpec(
            num_scalar_prefetch=1,
            grid=(1,),
            in_specs=[
                pl.BlockSpec((seq_len, 128), lambda g, index: (0, index[0])),
                whole(twist.shape),
                whole(forward.shape),
            ],
            out_specs=whole((blocks * width, 2 * rows)),
            scratch_shapes=[pltpu.VMEM((blocks, 128, rows), f32)],
        ),
    )
    result = call(
        mix_kernel,
        shape((blocks, 3 * width, rows), bf16),
        received, taps_values, twist, forward, backward,
        scratch_shapes=[pltpu.VMEM((3, blocks * width, 2 * rows), f32)],
    )
    back = lax.all_to_all(result, "ctx", 0, 0, tiled=True)
    lags = call(lags_kernel, shape((owners, rows // owners, channels), f32), back)
    arrived = lax.all_to_all(lags, "ch", 0, 0, tiled=True)
    out = shape((rows, channels), bf16)
    gates = call(gates_kernel, (out,) * 4, back, out_gate, in_gate, values, upstream)
    grad_filter = call(join_kernel, shape((rows // owners, owners * channels), f32), arrived)
    return (*gates, grad_filter)


def solution(mesh):
    return jax.shard_map(
        body,
        mesh=mesh,
        in_specs=(P("ctx", "ch"), P("ctx", "ch"), P("ctx", "ch"), P(None, "ch"), P("ctx", "ch")),
        out_specs=(
            P("ctx", "ch"),
            P("ctx", "ch"),
            P("ctx", "ch"),
            P("ctx", "ch"),
            P(("ctx", "ch"), None),
        ),
        check_vma=False,
    )
```

```python
import math

import jax
import jax.numpy as jnp
import ml_dtypes
import numpy as np
from jax import lax
from jax.experimental import pallas as pl
from jax.experimental.pallas import tpu as pltpu
from jax.sharding import PartitionSpec as P

VMEM = 48 * 1024 * 1024
PARTS = 2
f32, bf16 = jnp.float32, jnp.bfloat16


def leaf_angles(count, theta):
    if count == 1:
        return [theta]
    return leaf_angles(count // 2, theta / 2) + leaf_angles(count // 2, theta / 2 + math.pi)


def evaluate(coefs, theta):
    if len(coefs) == 1:
        return coefs
    half = len(coefs) // 2
    wr, wi = math.cos(theta / 2), math.sin(theta / 2)
    plus, minus = [], []
    for (lr, li), (hr, hi) in zip(coefs[:half], coefs[half:]):
        if hi is None:
            tr, ti = hr * wr, hr * wi
            plus.append((lr + tr, ti))
            minus.append((lr - tr, -ti))
        else:
            tr, ti = hr * wr - hi * wi, hr * wi + hi * wr
            plus.append((lr + tr, li + ti))
            minus.append((lr - tr, li - ti))
    return evaluate(plus, theta / 2) + evaluate(minus, theta / 2 + math.pi)


def interpolate(values, theta, real):
    if len(values) == 1:
        return values
    half = len(values) // 2
    wr, wi = math.cos(theta / 2), math.sin(theta / 2)
    plus = interpolate(values[:half], theta / 2, False)
    minus = interpolate(values[half:], theta / 2 + math.pi, False)
    low, high = [], []
    for (pr, pi), (mr, mi) in zip(plus, minus):
        dr, di = pr - mr, pi - mi
        if real:
            low.append(pr + mr)
            high.append(dr * wr + di * wi)
        else:
            low.append((pr + mr, pi + mi))
            high.append((dr * wr + di * wi, di * wr - dr * wi))
    return low + high


def tables(blocks, outer):
    phi = np.array(leaf_angles(blocks, math.pi / 2))
    b = np.arange(outer)
    twist = np.exp(1j * phi[:, None] * b[None, :] / outer)
    twist = np.concatenate([twist.real, twist.imag], 0).astype(np.float32)
    w = np.exp(2j * np.pi * (np.outer(b, b) % outer) / outer)
    forward = np.block([[w.real, w.imag], [-w.imag, w.real]])
    v = np.conj(w) / (blocks * outer)
    backward = np.block([[v.real, v.imag], [-v.imag, v.real]])

    def split(m):
        top = m.astype(np.float32).astype(ml_dtypes.bfloat16)
        rest = (m - top.astype(np.float64)).astype(np.float32).astype(ml_dtypes.bfloat16)
        return np.stack([top, rest])

    return twist, split(forward), split(backward)


def accurate_dot(x, m_ref):
    top = x.astype(bf16)
    rest = (x - top.astype(f32)).astype(bf16)
    dot = lambda a, b: jnp.dot(a, b, preferred_element_type=f32)
    return dot(top, m_ref[0]) + (dot(rest, m_ref[0]) + dot(top, m_ref[1]))


def send_kernel(out_gate, in_gate, values, upstream, send, held, arrived):
    blocks, width = send.shape[0], send.shape[1] // 2
    rows, channels = out_gate.shape
    part = channels // PARTS
    sources = (in_gate, values, upstream, out_gate)

    def fetch(n, p):
        at = slice(p * part, (p + 1) * part)
        return pltpu.make_async_copy(sources[n].at[:, at], held.at[n, p], arrived.at[n, p])

    for p in range(PARTS):
        for n in range(4):
            fetch(n, p).start()
    for p in range(PARTS):
        first = p * part // width
        for s in range(2):
            fetch(2 * s, p).wait()
            fetch(2 * s + 1, p).wait()
            gated = (held[2 * s, p].astype(f32) * held[2 * s + 1, p].astype(f32)).astype(bf16)
            send[first : first + part // width, s * width : (s + 1) * width, :] = gated.T.reshape(
                part // width, width, rows
            )


def forward_part(load, twist, matrix, work, width, outer):
    blocks = twist.shape[0] // 2
    for g in range(width // 16):
        coefs = [(load(i, g), None) for i in range(blocks)]
        for k, (re, im) in enumerate(evaluate(coefs, math.pi / 2)):
            cr, ci = twist[k : k + 1, :], twist[blocks + k : blocks + k + 1, :]
            at = slice(k * width + 16 * g, k * width + 16 * g + 16)
            work[at, :outer] = re * cr - im * ci
            work[at, outer:] = re * ci + im * cr
    step = 128
    for r in range(0, blocks * width, step):
        work[r : r + step, :] = accurate_dot(work[r : r + step, :], matrix)


def taps_kernel(index, taps, twist, matrix, spectrum, turned):
    blocks, outer = twist.shape[0] // 2, twist.shape[1]
    width = spectrum.shape[0] // blocks
    for i in range(blocks):
        turned[i] = taps[i * outer : (i + 1) * outer, :].astype(f32).T
    start = pl.multiple_of(index[1], 16)

    def load(i, g):
        return turned[i, pl.ds(start + 16 * g, 16), :]

    forward_part(load, twist, matrix, spectrum, width, outer)


def mix_kernel(received, taps_values, twist, forward, backward, result, work):
    blocks, width, outer = received.shape[0], received.shape[1] // 2, received.shape[2]
    for s in range(2):
        forward_part(
            lambda i, g: received[i, s * width + 16 * g : s * width + 16 * g + 16, :].astype(f32),
            twist, forward, work.at[s], width, outer,
        )
    step = 128
    for r in range(0, blocks * width, step):
        at = slice(r, r + step)
        pr, pi = work[0, at, :outer], work[0, at, outer:]
        cr, ci = work[1, at, :outer], work[1, at, outer:]
        hr, hi = taps_values[at, :outer], taps_values[at, outer:]
        filtered = jnp.concatenate([hr * pr - hi * pi, hr * pi + hi * pr], 1)
        mixed = jnp.concatenate([cr * hr + ci * hi, ci * hr - cr * hi], 1)
        lags = jnp.concatenate([cr * pr + ci * pi, ci * pr - cr * pi], 1)
        work[0, at, :] = accurate_dot(filtered, backward)
        work[1, at, :] = accurate_dot(mixed, backward)
        work[2, at, :] = accurate_dot(lags, backward)
    norm_factor = (blocks * outer) ** -0.5
    for s in range(3):
        for g in range(width // 16):
            values = []
            for k in range(blocks):
                cr, ci = twist[k : k + 1, :], twist[blocks + k : blocks + k + 1, :]
                at = slice(k * width + 16 * g, k * width + 16 * g + 16)
                re, im = work[s, at, :outer], work[s, at, outer:]
                values.append((re * cr + im * ci, im * cr - re * ci))
            for i, x in enumerate(interpolate(values, math.pi / 2, True)):
                if s == 2:
                    x = x * norm_factor
                result[i, s * width + 16 * g : s * width + 16 * g + 16, :] = x.astype(bf16)


def lags_kernel(back, lags):
    width = back.shape[1] // 3
    part = back[:, 2 * width :, :].astype(f32)
    turned = part.reshape(part.shape[0] * width, part.shape[2]).T
    lags[...] = turned.reshape(lags.shape).astype(bf16)


def gates_kernel(back, out_gate, in_gate, values, upstream, mixed_out, d_out_gate, d_in_gate, d_values):
    width = back.shape[1] // 3
    rows = back.shape[2]

    def part(s):
        x = back[:, s * width : (s + 1) * width, :].astype(f32)
        return x.reshape(x.shape[0] * width, rows).T

    filtered, grad_mixed = part(0), part(1)
    mixed_out[...] = (out_gate[...].astype(f32) * filtered).astype(bf16)
    d_out_gate[...] = (upstream[...].astype(f32) * filtered).astype(bf16)
    d_in_gate[...] = (grad_mixed * values[...].astype(f32)).astype(bf16)
    d_values[...] = (grad_mixed * in_gate[...].astype(f32)).astype(bf16)


def join_kernel(arrived, grad_filter):
    span = arrived.shape[2]
    for j in range(arrived.shape[0]):
        grad_filter[:, j * span : (j + 1) * span] = arrived[j].astype(f32)


def call(kernel, outs, *args, flops=1000000, vmem=VMEM, **kwargs):
    return pl.pallas_call(
        kernel,
        out_shape=outs,
        compiler_params=pltpu.CompilerParams(vmem_limit_bytes=vmem),
        cost_estimate=pl.CostEstimate(flops=flops, bytes_accessed=1 << 20, transcendentals=0),
        **kwargs,
    )(*args)


def body(out_gate, in_gate, values, filter_taps, upstream):
    rows, channels = out_gate.shape
    seq_len = filter_taps.shape[0]
    blocks = lax.axis_size("ctx")
    owners = lax.axis_size("ch")
    width = channels // blocks
    shape = jax.ShapeDtypeStruct
    twist, forward, backward = (jnp.asarray(t) for t in tables(blocks, rows))

    send = call(
        send_kernel,
        shape((blocks, 2 * width, rows), bf16),
        out_gate, in_gate, values, upstream,
        vmem=63 * 1024 * 1024 + 960 * 1024,
        in_specs=[pl.BlockSpec(memory_space=pltpu.HBM)] * 4,
        scratch_shapes=[
            pltpu.VMEM((4, PARTS, rows, channels // PARTS), bf16),
            pltpu.SemaphoreType.DMA((4, PARTS)),
        ],
    )
    received = lax.all_to_all(send, "ctx", 0, 0, tiled=True)

    me = lax.axis_index("ctx")
    first = me * width
    index = jnp.stack([first // 128, first % 128]).astype(jnp.int32)
    whole = lambda s: pl.BlockSpec(s, lambda g, index: (0,) * len(s))
    taps_values = call(
        taps_kernel,
        shape((blocks * width, 2 * rows), f32),
        index, filter_taps, twist, forward,
        grid_spec=pltpu.PrefetchScalarGridSpec(
            num_scalar_prefetch=1,
            grid=(1,),
            in_specs=[
                pl.BlockSpec((seq_len, 128), lambda g, index: (0, index[0])),
                whole(twist.shape),
                whole(forward.shape),
            ],
            out_specs=whole((blocks * width, 2 * rows)),
            scratch_shapes=[pltpu.VMEM((blocks, 128, rows), f32)],
        ),
    )
    result = call(
        mix_kernel,
        shape((blocks, 3 * width, rows), bf16),
        received, taps_values, twist, forward, backward,
        scratch_shapes=[pltpu.VMEM((3, blocks * width, 2 * rows), f32)],
    )
    back = lax.all_to_all(result, "ctx", 0, 0, tiled=True)
    lags = call(lags_kernel, shape((owners, rows // owners, channels), bf16), back)
    arrived = lax.all_to_all(lags, "ch", 0, 0, tiled=True)
    out = shape((rows, channels), bf16)
    gates = call(gates_kernel, (out,) * 4, back, out_gate, in_gate, values, upstream)
    grad_filter = call(join_kernel, shape((rows // owners, owners * channels), f32), arrived)
    return (*gates, grad_filter)


def solution(mesh):
    return jax.shard_map(
        body,
        mesh=mesh,
        in_specs=(P("ctx", "ch"), P("ctx", "ch"), P("ctx", "ch"), P(None, "ch"), P("ctx", "ch")),
        out_specs=(
            P("ctx", "ch"),
            P("ctx", "ch"),
            P("ctx", "ch"),
            P("ctx", "ch"),
            P(("ctx", "ch"), None),
        ),
        check_vma=False,
    )
```

```python
import math

import jax
import jax.numpy as jnp
import ml_dtypes
import numpy as np
from jax import lax
from jax.experimental import pallas as pl
from jax.experimental.pallas import tpu as pltpu
from jax.sharding import PartitionSpec as P

VMEM = 48 * 1024 * 1024
PARTS = 2
GROUP = 4
f32, bf16 = jnp.float32, jnp.bfloat16


def leaf_angles(count, theta):
    if count == 1:
        return [theta]
    return leaf_angles(count // 2, theta / 2) + leaf_angles(count // 2, theta / 2 + math.pi)


def evaluate(coefs, theta):
    if len(coefs) == 1:
        return coefs
    half = len(coefs) // 2
    wr, wi = math.cos(theta / 2), math.sin(theta / 2)
    plus, minus = [], []
    for (lr, li), (hr, hi) in zip(coefs[:half], coefs[half:]):
        if hi is None:
            tr, ti = hr * wr, hr * wi
            plus.append((lr + tr, ti))
            minus.append((lr - tr, -ti))
        else:
            tr, ti = hr * wr - hi * wi, hr * wi + hi * wr
            plus.append((lr + tr, li + ti))
            minus.append((lr - tr, li - ti))
    return evaluate(plus, theta / 2) + evaluate(minus, theta / 2 + math.pi)


def interpolate(values, theta, real):
    if len(values) == 1:
        return values
    half = len(values) // 2
    wr, wi = math.cos(theta / 2), math.sin(theta / 2)
    plus = interpolate(values[:half], theta / 2, False)
    minus = interpolate(values[half:], theta / 2 + math.pi, False)
    low, high = [], []
    for (pr, pi), (mr, mi) in zip(plus, minus):
        dr, di = pr - mr, pi - mi
        if real:
            low.append(pr + mr)
            high.append(dr * wr + di * wi)
        else:
            low.append((pr + mr, pi + mi))
            high.append((dr * wr + di * wi, di * wr - dr * wi))
    return low + high


def tables(blocks, outer):
    phi = np.array(leaf_angles(blocks, math.pi / 2))
    b = np.arange(outer)
    twist = np.exp(1j * phi[:, None] * b[None, :] / outer)
    twist = np.concatenate([twist.real, twist.imag], 0).astype(np.float32)
    w = np.exp(2j * np.pi * (np.outer(b, b) % outer) / outer)
    forward = np.block([[w.real, w.imag], [-w.imag, w.real]])
    v = np.conj(w) / (blocks * outer)
    backward = np.block([[v.real, v.imag], [-v.imag, v.real]])

    def split(m):
        top = m.astype(np.float32).astype(ml_dtypes.bfloat16)
        rest = (m - top.astype(np.float64)).astype(np.float32).astype(ml_dtypes.bfloat16)
        return np.stack([top, rest])

    return twist, split(forward), split(backward)


def accurate_dot(x, m_ref):
    top = x.astype(bf16)
    rest = (x - top.astype(f32)).astype(bf16)
    dot = lambda a, b: jnp.dot(a, b, preferred_element_type=f32)
    return dot(top, m_ref[0]) + (dot(rest, m_ref[0]) + dot(top, m_ref[1]))


def send_kernel(out_gate, in_gate, values, upstream, send, held, arrived):
    blocks, width = send.shape[0], send.shape[1] // 2
    rows, channels = out_gate.shape
    part = channels // PARTS
    sources = (in_gate, values, upstream, out_gate)

    def fetch(n, p):
        at = slice(p * part, (p + 1) * part)
        return pltpu.make_async_copy(sources[n].at[:, at], held.at[n, p], arrived.at[n, p])

    for p in range(PARTS):
        for n in range(4):
            fetch(n, p).start()
    for p in range(PARTS):
        first = p * part // width
        for s in range(2):
            fetch(2 * s, p).wait()
            fetch(2 * s + 1, p).wait()
            gated = (held[2 * s, p].astype(f32) * held[2 * s + 1, p].astype(f32)).astype(bf16)
            send[first : first + part // width, s * width : (s + 1) * width, :] = gated.T.reshape(
                part // width, width, rows
            )


def forward_part(load, twist, matrix, work, width, outer):
    blocks = twist.shape[0] // 2
    for g in range(width // 16):
        coefs = [(load(i, g), None) for i in range(blocks)]
        for k, (re, im) in enumerate(evaluate(coefs, math.pi / 2)):
            cr, ci = twist[k : k + 1, :], twist[blocks + k : blocks + k + 1, :]
            at = slice(k * width + 16 * g, k * width + 16 * g + 16)
            work[at, :outer] = re * cr - im * ci
            work[at, outer:] = re * ci + im * cr
    step = 128
    for r in range(0, blocks * width, step):
        work[r : r + step, :] = accurate_dot(work[r : r + step, :], matrix)


def taps_kernel(index, taps, twist, matrix, spectrum, turned):
    blocks, outer = twist.shape[0] // 2, twist.shape[1]
    width = spectrum.shape[0] // blocks
    for i in range(blocks):
        turned[i] = taps[i * outer : (i + 1) * outer, :].astype(f32).T
    start = pl.multiple_of(index[1], 16)

    def load(i, g):
        return turned[i, pl.ds(start + 16 * g, 16), :]

    forward_part(load, twist, matrix, spectrum, width, outer)


def swap_groups(parts):
    lane = lax.broadcasted_iota(jnp.int32, parts[0].shape, 1)
    low, even = lane < 64, lane // 32 % 2 == 0
    p0, p1, p2, p3 = parts
    p0, p2 = jnp.where(low, p0, pltpu.roll(p2, 64, 1)), jnp.where(low, pltpu.roll(p0, 64, 1), p2)
    p1, p3 = jnp.where(low, p1, pltpu.roll(p3, 64, 1)), jnp.where(low, pltpu.roll(p1, 64, 1), p3)
    p0, p1 = jnp.where(even, p0, pltpu.roll(p1, 32, 1)), jnp.where(even, pltpu.roll(p0, 96, 1), p1)
    p2, p3 = jnp.where(even, p2, pltpu.roll(p3, 32, 1)), jnp.where(even, pltpu.roll(p2, 96, 1), p3)
    return p0, p1, p2, p3


def mix_kernel(
    received, taps_values, twist, forward, backward,
    lag_send, near0, near1, near2, near3, work, result, lags, turned,
):
    blocks, width, outer = received.shape[0], received.shape[1] // 2, received.shape[2]
    for s in range(2):
        forward_part(
            lambda i, g: received[i, s * width + 16 * g : s * width + 16 * g + 16, :].astype(f32),
            twist, forward, work.at[s], width, outer,
        )
    step = 128
    for r in range(0, blocks * width, step):
        at = slice(r, r + step)
        pr, pi = work[0, at, :outer], work[0, at, outer:]
        cr, ci = work[1, at, :outer], work[1, at, outer:]
        hr, hi = taps_values[at, :outer], taps_values[at, outer:]
        filtered = jnp.concatenate([hr * pr - hi * pi, hr * pi + hi * pr], 1)
        mixed = jnp.concatenate([cr * hr + ci * hi, ci * hr - cr * hi], 1)
        lagged = jnp.concatenate([cr * pr + ci * pi, ci * pr - cr * pi], 1)
        work[0, at, :] = accurate_dot(filtered, backward)
        work[1, at, :] = accurate_dot(mixed, backward)
        work[2, at, :] = accurate_dot(lagged, backward)
    norm_factor = (blocks * outer) ** -0.5
    for s in range(3):
        for g in range(width // 16):
            values = []
            for k in range(blocks):
                cr, ci = twist[k : k + 1, :], twist[blocks + k : blocks + k + 1, :]
                at = slice(k * width + 16 * g, k * width + 16 * g + 16)
                re, im = work[s, at, :outer], work[s, at, outer:]
                values.append((re * cr + im * ci, im * cr - re * ci))
            for i, x in enumerate(interpolate(values, math.pi / 2, True)):
                if s == 2:
                    lags[i * width + 16 * g : i * width + 16 * g + 16, :] = x * norm_factor
                else:
                    result[i, s * width + 16 * g : s * width + 16 * g + 16, :] = x.astype(bf16)
    for m in range(blocks // GROUP):
        turned[m] = lags[m * 128 : (m + 1) * 128, :].T
        quarters = [turned[m, pl.ds(n, outer // GROUP, stride=GROUP), :] for n in range(GROUP)]
        for n, x in enumerate(swap_groups(quarters)):
            row = (m * GROUP + n) * (outer // GROUP)
            lag_send[row : row + outer // GROUP, :] = x.astype(bf16)
    place = lax.rem(lax.axis_index("ctx"), GROUP)
    for d, near in enumerate((near0, near1, near2, near3)):
        for x in range(GROUP):
            near[x] = result[GROUP * x + (place ^ d)]


def gates_kernel(
    far0, far1, far2, far3, out_gate, in_gate, values, upstream,
    mixed_out, d_out_gate, d_in_gate, d_values,
):
    width = far0.shape[1] // 2
    span = GROUP * width
    me = lax.axis_index("ctx")
    column, place = lax.div(me, GROUP), lax.rem(me, GROUP)
    for d, far in enumerate((far0, far1, far2, far3)):
        first = pl.multiple_of(lax.rem(column + GROUP - d, GROUP) * span, span)
        at = pl.ds(first, span)

        def part(s):
            x = [far[place ^ h, s * width : (s + 1) * width, :] for h in range(GROUP)]
            return jnp.concatenate(x, 0).astype(f32).T

        filtered, grad_mixed = part(0), part(1)
        mixed_out[:, at] = (out_gate[:, at].astype(f32) * filtered).astype(bf16)
        d_out_gate[:, at] = (upstream[:, at].astype(f32) * filtered).astype(bf16)
        d_in_gate[:, at] = (grad_mixed * values[:, at].astype(f32)).astype(bf16)
        d_values[:, at] = (grad_mixed * in_gate[:, at].astype(f32)).astype(bf16)


def join_kernel(arrived, grad_filter, turned):
    quads, lag_rows = turned.shape[0], grad_filter.shape[0]
    channels = quads * 128
    owners = grad_filter.shape[1] // channels
    count = owners * lag_rows // GROUP
    for m in range(quads):
        quarters = []
        for n in range(GROUP):
            row = (m * GROUP + n) * count
            quarters.append(arrived[row : row + count, :].astype(f32))
        for n, x in enumerate(swap_groups(quarters)):
            turned[m, pl.ds(n, count, stride=GROUP), :] = x
        for j in range(owners):
            first = j * channels + m * 128
            grad_filter[:, first : first + 128] = turned[m, j * lag_rows : (j + 1) * lag_rows, :]


def call(kernel, outs, *args, flops=1000000, vmem=VMEM, **kwargs):
    return pl.pallas_call(
        kernel,
        out_shape=outs,
        compiler_params=pltpu.CompilerParams(vmem_limit_bytes=vmem),
        cost_estimate=pl.CostEstimate(flops=flops, bytes_accessed=1 << 20, transcendentals=0),
        **kwargs,
    )(*args)


def body(out_gate, in_gate, values, filter_taps, upstream):
    rows, channels = out_gate.shape
    seq_len = filter_taps.shape[0]
    blocks = lax.axis_size("ctx")
    owners = lax.axis_size("ch")
    width = channels // blocks
    shape = jax.ShapeDtypeStruct
    twist, forward, backward = (jnp.asarray(t) for t in tables(blocks, rows))

    send = call(
        send_kernel,
        shape((blocks, 2 * width, rows), bf16),
        out_gate, in_gate, values, upstream,
        vmem=63 * 1024 * 1024 + 960 * 1024,
        in_specs=[pl.BlockSpec(memory_space=pltpu.HBM)] * 4,
        scratch_shapes=[
            pltpu.VMEM((4, PARTS, rows, channels // PARTS), bf16),
            pltpu.SemaphoreType.DMA((4, PARTS)),
        ],
    )
    received = lax.all_to_all(send, "ctx", 0, 0, tiled=True)

    me = lax.axis_index("ctx")
    first = me * width
    index = jnp.stack([first // 128, first % 128]).astype(jnp.int32)
    whole = lambda s: pl.BlockSpec(s, lambda g, index: (0,) * len(s))
    taps_values = call(
        taps_kernel,
        shape((blocks * width, 2 * rows), f32),
        index, filter_taps, twist, forward,
        grid_spec=pltpu.PrefetchScalarGridSpec(
            num_scalar_prefetch=1,
            grid=(1,),
            in_specs=[
                pl.BlockSpec((seq_len, 128), lambda g, index: (0, index[0])),
                whole(twist.shape),
                whole(forward.shape),
            ],
            out_specs=whole((blocks * width, 2 * rows)),
            scratch_shapes=[pltpu.VMEM((blocks, 128, rows), f32)],
        ),
    )
    chunk = shape((GROUP, 2 * width, rows), bf16)
    lag_send, *near = call(
        mix_kernel,
        (shape((blocks * rows // GROUP, 128), bf16),) + (chunk,) * GROUP,
        received, taps_values, twist, forward, backward,
        scratch_shapes=[
            pltpu.VMEM((3, blocks * width, 2 * rows), f32),
            pltpu.VMEM((blocks, 2 * width, rows), bf16),
            pltpu.VMEM((blocks * width, rows), f32),
            pltpu.VMEM((blocks // GROUP, rows, 128), f32),
        ],
    )
    lag_rows = rows // owners
    chunks = lag_send.reshape(blocks * owners, lag_rows // GROUP, 128)
    arrived = lax.all_to_all(chunks, ("ctx", "ch"), 0, 0, tiled=True).reshape(lag_send.shape)

    near = near[:1] + [
        lax.ppermute(near[d], "ctx", [(i, i ^ d) for i in range(blocks)]) for d in range(1, GROUP)
    ]
    near = jnp.stack(near)
    far = [
        lax.dynamic_index_in_dim(near, (me // GROUP + d) % GROUP, 1, keepdims=False)
        for d in range(GROUP)
    ]
    far = far[:1] + [
        lax.ppermute(far[d], "ctx", [(i, (i + GROUP * d) % blocks) for i in range(blocks)])
        for d in range(1, GROUP)
    ]
    out = shape((rows, channels), bf16)
    gates = call(gates_kernel, (out,) * 4, *far, out_gate, in_gate, values, upstream)
    grad_filter = call(
        join_kernel,
        shape((lag_rows, owners * channels), f32),
        arrived,
        scratch_shapes=[pltpu.VMEM((channels // 128, rows, 128), f32)],
    )
    return (*gates, grad_filter)


def solution(mesh):
    return jax.shard_map(
        body,
        mesh=mesh,
        in_specs=(P("ctx", "ch"), P("ctx", "ch"), P("ctx", "ch"), P(None, "ch"), P("ctx", "ch")),
        out_specs=(
            P("ctx", "ch"),
            P("ctx", "ch"),
            P("ctx", "ch"),
            P("ctx", "ch"),
            P(("ctx", "ch"), None),
        ),
        check_vma=False,
    )
```

```python
import math

import jax
import jax.numpy as jnp
import ml_dtypes
import numpy as np
from jax import lax
from jax.experimental import pallas as pl
from jax.experimental.pallas import tpu as pltpu
from jax.sharding import PartitionSpec as P

VMEM = 48 * 1024 * 1024
PARTS = 2
GROUP = 4
f32, bf16 = jnp.float32, jnp.bfloat16


def leaf_angles(count, theta):
    if count == 1:
        return [theta]
    return leaf_angles(count // 2, theta / 2) + leaf_angles(count // 2, theta / 2 + math.pi)


def evaluate(coefs, theta):
    if len(coefs) == 1:
        return coefs
    half = len(coefs) // 2
    wr, wi = math.cos(theta / 2), math.sin(theta / 2)
    plus, minus = [], []
    for (lr, li), (hr, hi) in zip(coefs[:half], coefs[half:]):
        if hi is None:
            tr, ti = hr * wr, hr * wi
            plus.append((lr + tr, ti))
            minus.append((lr - tr, -ti))
        else:
            tr, ti = hr * wr - hi * wi, hr * wi + hi * wr
            plus.append((lr + tr, li + ti))
            minus.append((lr - tr, li - ti))
    return evaluate(plus, theta / 2) + evaluate(minus, theta / 2 + math.pi)


def interpolate(values, theta, real):
    if len(values) == 1:
        return values
    half = len(values) // 2
    wr, wi = math.cos(theta / 2), math.sin(theta / 2)
    plus = interpolate(values[:half], theta / 2, False)
    minus = interpolate(values[half:], theta / 2 + math.pi, False)
    low, high = [], []
    for (pr, pi), (mr, mi) in zip(plus, minus):
        dr, di = pr - mr, pi - mi
        if real:
            low.append(pr + mr)
            high.append(dr * wr + di * wi)
        else:
            low.append((pr + mr, pi + mi))
            high.append((dr * wr + di * wi, di * wr - dr * wi))
    return low + high


def tables(blocks, outer):
    phi = np.array(leaf_angles(blocks, math.pi / 2))
    b = np.arange(outer)
    twist = np.exp(1j * phi[:, None] * b[None, :] / outer)
    twist = np.concatenate([twist.real, twist.imag], 0).astype(np.float32)
    w = np.exp(2j * np.pi * (np.outer(b, b) % outer) / outer)
    forward = np.block([[w.real, w.imag], [-w.imag, w.real]])
    v = np.conj(w) / (blocks * outer)
    backward = np.block([[v.real, v.imag], [-v.imag, v.real]])

    def split(m):
        top = m.astype(np.float32).astype(ml_dtypes.bfloat16)
        rest = (m - top.astype(np.float64)).astype(np.float32).astype(ml_dtypes.bfloat16)
        return np.stack([top, rest])

    return twist, split(forward), split(backward)


def accurate_dot(x, m_ref):
    top = x.astype(bf16)
    rest = (x - top.astype(f32)).astype(bf16)
    dot = lambda a, b: jnp.dot(a, b, preferred_element_type=f32)
    return dot(top, m_ref[0]) + (dot(rest, m_ref[0]) + dot(top, m_ref[1]))


def send_kernel(out_gate, in_gate, values, upstream, send, held, arrived, ready, sent):
    blocks, width = send.shape[0], send.shape[1] // 2
    rows, channels = out_gate.shape
    part = channels // PARTS
    sources = (in_gate, values, upstream, out_gate)

    def fetch(n, p):
        at = slice(p * part, (p + 1) * part)
        return pltpu.make_async_copy(sources[n].at[:, at], held.at[n, p], arrived.at[n, p])

    def leave(p):
        at = slice(p * part // width, (p + 1) * part // width)
        return pltpu.make_async_copy(ready.at[at], send.at[at], sent.at[p])

    for p in range(PARTS):
        for n in range(4):
            fetch(n, p).start()
    for p in range(PARTS):
        first = p * part // width
        for s in range(2):
            fetch(2 * s, p).wait()
            fetch(2 * s + 1, p).wait()
            gated = (held[2 * s, p].astype(f32) * held[2 * s + 1, p].astype(f32)).astype(bf16)
            ready[first : first + part // width, s * width : (s + 1) * width, :] = gated.T.reshape(
                part // width, width, rows
            )
        leave(p).start()
    for p in range(PARTS):
        leave(p).wait()


def forward_part(load, twist, matrix, work, width, outer):
    blocks = twist.shape[0] // 2
    for g in range(width // 16):
        coefs = [(load(i, g), None) for i in range(blocks)]
        for k, (re, im) in enumerate(evaluate(coefs, math.pi / 2)):
            cr, ci = twist[k : k + 1, :], twist[blocks + k : blocks + k + 1, :]
            at = slice(k * width + 16 * g, k * width + 16 * g + 16)
            work[at, :outer] = re * cr - im * ci
            work[at, outer:] = re * ci + im * cr
    step = 128
    for r in range(0, blocks * width, step):
        work[r : r + step, :] = accurate_dot(work[r : r + step, :], matrix)


def taps_kernel(index, taps, twist, matrix, spectrum, turned):
    blocks, outer = twist.shape[0] // 2, twist.shape[1]
    width = spectrum.shape[0] // blocks
    for i in range(blocks):
        turned[i] = taps[i * outer : (i + 1) * outer, :].astype(f32).T
    start = pl.multiple_of(index[1], 16)

    def load(i, g):
        return turned[i, pl.ds(start + 16 * g, 16), :]

    forward_part(load, twist, matrix, spectrum, width, outer)


def swap_groups(parts):
    lane = lax.broadcasted_iota(jnp.int32, parts[0].shape, 1)
    low, even = lane < 64, lane // 32 % 2 == 0
    p0, p1, p2, p3 = parts
    p0, p2 = jnp.where(low, p0, pltpu.roll(p2, 64, 1)), jnp.where(low, pltpu.roll(p0, 64, 1), p2)
    p1, p3 = jnp.where(low, p1, pltpu.roll(p3, 64, 1)), jnp.where(low, pltpu.roll(p1, 64, 1), p3)
    p0, p1 = jnp.where(even, p0, pltpu.roll(p1, 32, 1)), jnp.where(even, pltpu.roll(p0, 96, 1), p1)
    p2, p3 = jnp.where(even, p2, pltpu.roll(p3, 32, 1)), jnp.where(even, pltpu.roll(p2, 96, 1), p3)
    return p0, p1, p2, p3


def mix_kernel(
    received, taps_values, twist, forward, backward,
    lag_send, near0, near1, work, result, lags, turned, packed, done,
):
    blocks, width, outer = received.shape[0], received.shape[1] // 2, received.shape[2]
    for s in range(2):
        forward_part(
            lambda i, g: received[i, s * width + 16 * g : s * width + 16 * g + 16, :].astype(f32),
            twist, forward, work.at[s], width, outer,
        )
    step = 128
    for r in range(0, blocks * width, step):
        at = slice(r, r + step)
        pr, pi = work[0, at, :outer], work[0, at, outer:]
        cr, ci = work[1, at, :outer], work[1, at, outer:]
        hr, hi = taps_values[at, :outer], taps_values[at, outer:]
        filtered = jnp.concatenate([hr * pr - hi * pi, hr * pi + hi * pr], 1)
        mixed = jnp.concatenate([cr * hr + ci * hi, ci * hr - cr * hi], 1)
        lagged = jnp.concatenate([cr * pr + ci * pi, ci * pr - cr * pi], 1)
        work[0, at, :] = accurate_dot(filtered, backward)
        work[1, at, :] = accurate_dot(mixed, backward)
        work[2, at, :] = accurate_dot(lagged, backward)
    norm_factor = (blocks * outer) ** -0.5
    def inverse(s, store):
        for g in range(width // 16):
            values = []
            for k in range(blocks):
                cr, ci = twist[k : k + 1, :], twist[blocks + k : blocks + k + 1, :]
                at = slice(k * width + 16 * g, k * width + 16 * g + 16)
                re, im = work[s, at, :outer], work[s, at, outer:]
                values.append((re * cr + im * ci, im * cr - re * ci))
            for i, x in enumerate(interpolate(values, math.pi / 2, True)):
                store(i, slice(16 * g, 16 * g + 16), x)

    def keep_lags(i, at, x):
        lags[i * width + at.start : i * width + at.stop, :] = x * norm_factor

    inverse(2, keep_lags)
    for m in range(blocks // GROUP):
        turned[m] = lags[m * 128 : (m + 1) * 128, :].T
        quarters = [turned[m, pl.ds(n, outer // GROUP, stride=GROUP), :] for n in range(GROUP)]
        for n, x in enumerate(swap_groups(quarters)):
            row = (m * GROUP + n) * (outer // GROUP)
            packed[row : row + outer // GROUP, :] = x.astype(bf16)
    out = pltpu.make_async_copy(packed, lag_send, done)
    out.start()

    @pl.loop(0, 2)
    def _(s):
        def keep(i, at, x):
            result[s, i, at, :] = x.astype(bf16)

        inverse(s, keep)

    place = lax.rem(lax.axis_index("ctx"), GROUP)
    for k, near in enumerate((near0, near1)):
        for e in range(2):
            for x in range(GROUP):
                for s in range(2):
                    source = result[s, GROUP * x + (place ^ (2 * k + e))]
                    near[e, x, s * width : (s + 1) * width, :] = source
    out.wait()


def turn_kernel(stay, came, crossed, far0, far1, far2, far3):
    column = lax.div(lax.axis_index("ctx"), GROUP)
    for d, far in enumerate((far0, far1, far2, far3)):
        x = lax.rem(column + d, GROUP)
        far[0], far[1] = stay[0, x], came[0, x]
        far[2], far[3] = crossed[0, x], crossed[1, x]


def gates_kernel(
    far0, far1, far2, far3, out_gate, in_gate, values, upstream,
    mixed_out, d_out_gate, d_in_gate, d_values,
):
    width = far0.shape[1] // 2
    span = GROUP * width
    me = lax.axis_index("ctx")
    column, place = lax.div(me, GROUP), lax.rem(me, GROUP)
    slot = lambda e: lax.rem(e, 2) * 2 + lax.div(e, 2)
    for d, far in enumerate((far0, far1, far2, far3)):
        first = pl.multiple_of(lax.rem(column + GROUP - d, GROUP) * span, span)
        at = pl.ds(first, span)

        def part(s):
            x = [far[slot(place ^ h), s * width : (s + 1) * width, :] for h in range(GROUP)]
            return jnp.concatenate(x, 0).astype(f32).T

        filtered, grad_mixed = part(0), part(1)
        mixed_out[:, at] = (out_gate[:, at].astype(f32) * filtered).astype(bf16)
        d_out_gate[:, at] = (upstream[:, at].astype(f32) * filtered).astype(bf16)
        d_in_gate[:, at] = (grad_mixed * values[:, at].astype(f32)).astype(bf16)
        d_values[:, at] = (grad_mixed * in_gate[:, at].astype(f32)).astype(bf16)


def join_kernel(arrived, grad_filter, turned):
    quads, lag_rows = turned.shape[0], grad_filter.shape[0]
    channels = quads * 128
    owners = grad_filter.shape[1] // channels
    count = owners * lag_rows // GROUP
    for m in range(quads):
        quarters = []
        for n in range(GROUP):
            row = (m * GROUP + n) * count
            quarters.append(arrived[row : row + count, :].astype(f32))
        for n, x in enumerate(swap_groups(quarters)):
            turned[m, pl.ds(n, count, stride=GROUP), :] = x
        for j in range(owners):
            first = j * channels + m * 128
            grad_filter[:, first : first + 128] = turned[m, j * lag_rows : (j + 1) * lag_rows, :]


def call(kernel, outs, *args, flops=1000000, vmem=VMEM, **kwargs):
    return pl.pallas_call(
        kernel,
        out_shape=outs,
        compiler_params=pltpu.CompilerParams(vmem_limit_bytes=vmem),
        cost_estimate=pl.CostEstimate(flops=flops, bytes_accessed=1 << 20, transcendentals=0),
        **kwargs,
    )(*args)


def body(out_gate, in_gate, values, filter_taps, upstream):
    rows, channels = out_gate.shape
    seq_len = filter_taps.shape[0]
    blocks = lax.axis_size("ctx")
    owners = lax.axis_size("ch")
    width = channels // blocks
    shape = jax.ShapeDtypeStruct
    twist, forward, backward = (jnp.asarray(t) for t in tables(blocks, rows))

    send = call(
        send_kernel,
        shape((blocks, 2 * width, rows), bf16),
        out_gate, in_gate, values, upstream,
        vmem=63 * 1024 * 1024 + 960 * 1024,
        in_specs=[pl.BlockSpec(memory_space=pltpu.HBM)] * 4,
        scratch_shapes=[
            pltpu.VMEM((4, PARTS, rows, channels // PARTS), bf16),
            pltpu.SemaphoreType.DMA((4, PARTS)),
            pltpu.VMEM((blocks, 2 * width, rows), bf16),
            pltpu.SemaphoreType.DMA((PARTS,)),
        ],
        out_specs=pl.BlockSpec(memory_space=pltpu.HBM),
    )
    received = lax.all_to_all(send, "ctx", 0, 0, tiled=True)

    me = lax.axis_index("ctx")
    first = me * width
    index = jnp.stack([first // 128, first % 128]).astype(jnp.int32)
    whole = lambda s: pl.BlockSpec(s, lambda g, index: (0,) * len(s))
    taps_values = call(
        taps_kernel,
        shape((blocks * width, 2 * rows), f32),
        index, filter_taps, twist, forward,
        grid_spec=pltpu.PrefetchScalarGridSpec(
            num_scalar_prefetch=1,
            grid=(1,),
            in_specs=[
                pl.BlockSpec((seq_len, 128), lambda g, index: (0, index[0])),
                whole(twist.shape),
                whole(forward.shape),
            ],
            out_specs=whole((blocks * width, 2 * rows)),
            scratch_shapes=[pltpu.VMEM((blocks, 128, rows), f32)],
        ),
    )
    near = shape((2, GROUP, 2 * width, rows), bf16)
    lag_send, stay, leave = call(
        mix_kernel,
        (shape((blocks * rows // GROUP, 128), bf16), near, near),
        received, taps_values, twist, forward, backward,
        scratch_shapes=[
            pltpu.VMEM((3, blocks * width, 2 * rows), f32),
            pltpu.VMEM((2, blocks, width, rows), bf16),
            pltpu.VMEM((blocks * width, rows), f32),
            pltpu.VMEM((blocks // GROUP, rows, 128), f32),
            pltpu.VMEM((blocks * rows // GROUP, 128), bf16),
            pltpu.SemaphoreType.DMA,
        ],
        out_specs=(pl.BlockSpec(memory_space=pltpu.HBM),) + (pl.BlockSpec(memory_space=pltpu.VMEM),) * 2,
    )
    lag_rows = rows // owners
    chunks = lag_send.reshape(blocks * owners, lag_rows // GROUP, 128)
    arrived = lax.all_to_all(chunks, ("ctx", "ch"), 0, 0, tiled=True).reshape(lag_send.shape)

    came = lax.ppermute(leave, "ctx", [(i, i ^ 2) for i in range(blocks)])
    cross = jnp.stack([stay[1], came[1]])
    crossed = lax.ppermute(cross, "ctx", [(i, i ^ 1) for i in range(blocks)])
    far = call(turn_kernel, (shape((GROUP, 2 * width, rows), bf16),) * GROUP, stay, came, crossed)
    far = list(far)
    far = far[:1] + [
        lax.ppermute(far[d], "ctx", [(i, (i + GROUP * d) % blocks) for i in range(blocks)])
        for d in range(1, GROUP)
    ]
    out = shape((rows, channels), bf16)
    gates = call(gates_kernel, (out,) * 4, *far, out_gate, in_gate, values, upstream)
    arrived, *gates = lax.optimization_barrier((arrived, *gates))
    grad_filter = call(
        join_kernel,
        shape((lag_rows, owners * channels), f32),
        arrived,
        scratch_shapes=[pltpu.VMEM((channels // 128, rows, 128), f32)],
    )
    return (*gates, grad_filter)


def solution(mesh):
    return jax.shard_map(
        body,
        mesh=mesh,
        in_specs=(P("ctx", "ch"), P("ctx", "ch"), P("ctx", "ch"), P(None, "ch"), P("ctx", "ch")),
        out_specs=(
            P("ctx", "ch"),
            P("ctx", "ch"),
            P("ctx", "ch"),
            P("ctx", "ch"),
            P(("ctx", "ch"), None),
        ),
        check_vma=False,
    )
```

```python
import math

import jax
import jax.numpy as jnp
import ml_dtypes
import numpy as np
from jax import lax
from jax.experimental import pallas as pl
from jax.experimental.pallas import tpu as pltpu
from jax.sharding import PartitionSpec as P

VMEM = 48 * 1024 * 1024
PARTS = 2
CTX_FIRST, CH_FIRST = 11, 9
f32, bf16 = jnp.float32, jnp.bfloat16


def slot(i, first, count):
    return (i - first) % count


def exchange(x, axis, first):
    count = lax.axis_size(axis)
    devices = [[(first + k) % count for k in range(count)]]
    return lax.all_to_all(x, axis, 0, 0, tiled=True, axis_index_groups=devices)


def leaf_angles(count, theta):
    if count == 1:
        return [theta]
    return leaf_angles(count // 2, theta / 2) + leaf_angles(count // 2, theta / 2 + math.pi)


def evaluate(coefs, theta):
    if len(coefs) == 1:
        return coefs
    half = len(coefs) // 2
    wr, wi = math.cos(theta / 2), math.sin(theta / 2)
    plus, minus = [], []
    for (lr, li), (hr, hi) in zip(coefs[:half], coefs[half:]):
        if hi is None:
            tr, ti = hr * wr, hr * wi
            plus.append((lr + tr, ti))
            minus.append((lr - tr, -ti))
        else:
            tr, ti = hr * wr - hi * wi, hr * wi + hi * wr
            plus.append((lr + tr, li + ti))
            minus.append((lr - tr, li - ti))
    return evaluate(plus, theta / 2) + evaluate(minus, theta / 2 + math.pi)


def interpolate(values, theta, real):
    if len(values) == 1:
        return values
    half = len(values) // 2
    wr, wi = math.cos(theta / 2), math.sin(theta / 2)
    plus = interpolate(values[:half], theta / 2, False)
    minus = interpolate(values[half:], theta / 2 + math.pi, False)
    low, high = [], []
    for (pr, pi), (mr, mi) in zip(plus, minus):
        dr, di = pr - mr, pi - mi
        if real:
            low.append(pr + mr)
            high.append(dr * wr + di * wi)
        else:
            low.append((pr + mr, pi + mi))
            high.append((dr * wr + di * wi, di * wr - dr * wi))
    return low + high


def tables(blocks, outer):
    phi = np.array(leaf_angles(blocks, math.pi / 2))
    b = np.arange(outer)
    twist = np.exp(1j * phi[:, None] * b[None, :] / outer)
    twist = np.concatenate([twist.real, twist.imag], 0).astype(np.float32)
    w = np.exp(2j * np.pi * (np.outer(b, b) % outer) / outer)
    forward = np.block([[w.real, w.imag], [-w.imag, w.real]])
    v = np.conj(w) / (blocks * outer)
    backward = np.block([[v.real, v.imag], [-v.imag, v.real]])

    def split(m):
        top = m.astype(np.float32).astype(ml_dtypes.bfloat16)
        rest = (m - top.astype(np.float64)).astype(np.float32).astype(ml_dtypes.bfloat16)
        return np.stack([top, rest])

    return twist, split(forward), split(backward)


def accurate_dot(x, m_ref):
    top = x.astype(bf16)
    rest = (x - top.astype(f32)).astype(bf16)
    dot = lambda a, b: jnp.dot(a, b, preferred_element_type=f32)
    return dot(top, m_ref[0]) + (dot(rest, m_ref[0]) + dot(top, m_ref[1]))


def send_kernel(out_gate, in_gate, values, upstream, send, held, arrived):
    blocks, width = send.shape[0], send.shape[1] // 2
    rows, channels = out_gate.shape
    part = channels // PARTS
    sources = (in_gate, values, upstream, out_gate)

    def fetch(n, p):
        at = slice(p * part, (p + 1) * part)
        return pltpu.make_async_copy(sources[n].at[:, at], held.at[n, p], arrived.at[n, p])

    for p in range(PARTS):
        for n in range(4):
            fetch(n, p).start()
    for p in range(PARTS):
        first = p * part // width
        for s in range(2):
            fetch(2 * s, p).wait()
            fetch(2 * s + 1, p).wait()
            gated = (held[2 * s, p].astype(f32) * held[2 * s + 1, p].astype(f32)).astype(bf16)
            turned = gated.T
            for n in range(part // width):
                at = slot(first + n, CTX_FIRST, blocks)
                send[at, s * width : (s + 1) * width, :] = turned[n * width : (n + 1) * width]


def forward_part(load, twist, matrix, work, width, outer):
    blocks = twist.shape[0] // 2
    for g in range(width // 16):
        coefs = [(load(i, g), None) for i in range(blocks)]
        for k, (re, im) in enumerate(evaluate(coefs, math.pi / 2)):
            cr, ci = twist[k : k + 1, :], twist[blocks + k : blocks + k + 1, :]
            at = slice(k * width + 16 * g, k * width + 16 * g + 16)
            work[at, :outer] = re * cr - im * ci
            work[at, outer:] = re * ci + im * cr
    step = 128
    for r in range(0, blocks * width, step):
        work[r : r + step, :] = accurate_dot(work[r : r + step, :], matrix)


def taps_kernel(index, taps, twist, matrix, spectrum, turned):
    blocks, outer = twist.shape[0] // 2, twist.shape[1]
    width = spectrum.shape[0] // blocks
    for i in range(blocks):
        turned[i] = taps[i * outer : (i + 1) * outer, :].astype(f32).T
    start = pl.multiple_of(index[1], 16)

    def load(i, g):
        return turned[i, pl.ds(start + 16 * g, 16), :]

    forward_part(load, twist, matrix, spectrum, width, outer)


def mix_kernel(received, taps_values, twist, forward, backward, result, work):
    blocks, width, outer = received.shape[0], received.shape[1] // 2, received.shape[2]
    for s in range(2):
        forward_part(
            lambda i, g: received[slot(i, CTX_FIRST, blocks), s * width + 16 * g : s * width + 16 * g + 16, :].astype(f32),
            twist, forward, work.at[s], width, outer,
        )
    step = 128
    for r in range(0, blocks * width, step):
        at = slice(r, r + step)
        pr, pi = work[0, at, :outer], work[0, at, outer:]
        cr, ci = work[1, at, :outer], work[1, at, outer:]
        hr, hi = taps_values[at, :outer], taps_values[at, outer:]
        filtered = jnp.concatenate([hr * pr - hi * pi, hr * pi + hi * pr], 1)
        mixed = jnp.concatenate([cr * hr + ci * hi, ci * hr - cr * hi], 1)
        lags = jnp.concatenate([cr * pr + ci * pi, ci * pr - cr * pi], 1)
        work[0, at, :] = accurate_dot(filtered, backward)
        work[1, at, :] = accurate_dot(mixed, backward)
        work[2, at, :] = accurate_dot(lags, backward)
    norm_factor = (blocks * outer) ** -0.5
    for s in range(3):
        for g in range(width // 16):
            values = []
            for k in range(blocks):
                cr, ci = twist[k : k + 1, :], twist[blocks + k : blocks + k + 1, :]
                at = slice(k * width + 16 * g, k * width + 16 * g + 16)
                re, im = work[s, at, :outer], work[s, at, outer:]
                values.append((re * cr + im * ci, im * cr - re * ci))
            for i, x in enumerate(interpolate(values, math.pi / 2, True)):
                if s == 2:
                    x = x * norm_factor
                result[slot(i, CTX_FIRST, blocks), s * width + 16 * g : s * width + 16 * g + 16, :] = x.astype(bf16)


def gather_part(back, s):
    width, blocks = back.shape[1] // 3, back.shape[0]
    parts = [back[slot(d, CTX_FIRST, blocks), s * width : (s + 1) * width, :] for d in range(blocks)]
    return jnp.concatenate(parts, 0).astype(f32).T


def lags_kernel(back, lags):
    turned = gather_part(back, 2)
    owners, rows = lags.shape[0], lags.shape[1]
    for j in range(owners):
        lags[slot(j, CH_FIRST, owners)] = turned[j * rows : (j + 1) * rows, :].astype(bf16)


def gates_kernel(back, out_gate, in_gate, values, upstream, mixed_out, d_out_gate, d_in_gate, d_values):
    filtered, grad_mixed = gather_part(back, 0), gather_part(back, 1)
    mixed_out[...] = (out_gate[...].astype(f32) * filtered).astype(bf16)
    d_out_gate[...] = (upstream[...].astype(f32) * filtered).astype(bf16)
    d_in_gate[...] = (grad_mixed * values[...].astype(f32)).astype(bf16)
    d_values[...] = (grad_mixed * in_gate[...].astype(f32)).astype(bf16)


def join_kernel(arrived, grad_filter):
    owners, span = arrived.shape[0], arrived.shape[2]
    for j in range(owners):
        at = slot(j, CH_FIRST, owners)
        grad_filter[:, j * span : (j + 1) * span] = arrived[at].astype(f32)


def call(kernel, outs, *args, flops=1000000, vmem=VMEM, **kwargs):
    return pl.pallas_call(
        kernel,
        out_shape=outs,
        compiler_params=pltpu.CompilerParams(vmem_limit_bytes=vmem),
        cost_estimate=pl.CostEstimate(flops=flops, bytes_accessed=1 << 20, transcendentals=0),
        **kwargs,
    )(*args)


def body(out_gate, in_gate, values, filter_taps, upstream):
    rows, channels = out_gate.shape
    seq_len = filter_taps.shape[0]
    blocks = lax.axis_size("ctx")
    owners = lax.axis_size("ch")
    width = channels // blocks
    shape = jax.ShapeDtypeStruct
    twist, forward, backward = (jnp.asarray(t) for t in tables(blocks, rows))

    send = call(
        send_kernel,
        shape((blocks, 2 * width, rows), bf16),
        out_gate, in_gate, values, upstream,
        vmem=63 * 1024 * 1024 + 960 * 1024,
        in_specs=[pl.BlockSpec(memory_space=pltpu.HBM)] * 4,
        scratch_shapes=[
            pltpu.VMEM((4, PARTS, rows, channels // PARTS), bf16),
            pltpu.SemaphoreType.DMA((4, PARTS)),
        ],
    )
    received = exchange(send, "ctx", CTX_FIRST)

    me = lax.axis_index("ctx")
    first = me * width
    index = jnp.stack([first // 128, first % 128]).astype(jnp.int32)
    whole = lambda s: pl.BlockSpec(s, lambda g, index: (0,) * len(s))
    taps_values = call(
        taps_kernel,
        shape((blocks * width, 2 * rows), f32),
        index, filter_taps, twist, forward,
        grid_spec=pltpu.PrefetchScalarGridSpec(
            num_scalar_prefetch=1,
            grid=(1,),
            in_specs=[
                pl.BlockSpec((seq_len, 128), lambda g, index: (0, index[0])),
                whole(twist.shape),
                whole(forward.shape),
            ],
            out_specs=whole((blocks * width, 2 * rows)),
            scratch_shapes=[pltpu.VMEM((blocks, 128, rows), f32)],
        ),
    )
    result = call(
        mix_kernel,
        shape((blocks, 3 * width, rows), bf16),
        received, taps_values, twist, forward, backward,
        scratch_shapes=[pltpu.VMEM((3, blocks * width, 2 * rows), f32)],
    )
    back = exchange(result, "ctx", CTX_FIRST)
    lags = call(lags_kernel, shape((owners, rows // owners, channels), bf16), back)
    arrived = exchange(lags, "ch", CH_FIRST)
    out = shape((rows, channels), bf16)
    gates = call(gates_kernel, (out,) * 4, back, out_gate, in_gate, values, upstream)
    grad_filter = call(join_kernel, shape((rows // owners, owners * channels), f32), arrived)
    return (*gates, grad_filter)


def solution(mesh):
    return jax.shard_map(
        body,
        mesh=mesh,
        in_specs=(P("ctx", "ch"), P("ctx", "ch"), P("ctx", "ch"), P(None, "ch"), P("ctx", "ch")),
        out_specs=(
            P("ctx", "ch"),
            P("ctx", "ch"),
            P("ctx", "ch"),
            P("ctx", "ch"),
            P(("ctx", "ch"), None),
        ),
        check_vma=False,
    )
```

```python
import math

import jax
import jax.numpy as jnp
import ml_dtypes
import numpy as np
from jax import lax
from jax.experimental import pallas as pl
from jax.experimental.pallas import tpu as pltpu
from jax.sharding import PartitionSpec as P

VMEM = 48 * 1024 * 1024
PARTS = 2
CTX_FIRST, CH_FIRST = 11, 9
f32, bf16 = jnp.float32, jnp.bfloat16


def slot(i, first, count):
    return (i - first) % count


def exchange(x, axis, first):
    count = lax.axis_size(axis)
    devices = [[(first + k) % count for k in range(count)]]
    return lax.all_to_all(x, axis, 0, 0, tiled=True, axis_index_groups=devices)


def leaf_angles(count, theta):
    if count == 1:
        return [theta]
    return leaf_angles(count // 2, theta / 2) + leaf_angles(count // 2, theta / 2 + math.pi)


def evaluate(coefs, theta):
    if len(coefs) == 1:
        return coefs
    half = len(coefs) // 2
    wr, wi = math.cos(theta / 2), math.sin(theta / 2)
    plus, minus = [], []
    for (lr, li), (hr, hi) in zip(coefs[:half], coefs[half:]):
        if hi is None:
            tr, ti = hr * wr, hr * wi
            plus.append((lr + tr, ti))
            minus.append((lr - tr, -ti))
        else:
            tr, ti = hr * wr - hi * wi, hr * wi + hi * wr
            plus.append((lr + tr, li + ti))
            minus.append((lr - tr, li - ti))
    return evaluate(plus, theta / 2) + evaluate(minus, theta / 2 + math.pi)


def interpolate(values, theta, real):
    if len(values) == 1:
        return values
    half = len(values) // 2
    wr, wi = math.cos(theta / 2), math.sin(theta / 2)
    plus = interpolate(values[:half], theta / 2, False)
    minus = interpolate(values[half:], theta / 2 + math.pi, False)
    low, high = [], []
    for (pr, pi), (mr, mi) in zip(plus, minus):
        dr, di = pr - mr, pi - mi
        if real:
            low.append(pr + mr)
            high.append(dr * wr + di * wi)
        else:
            low.append((pr + mr, pi + mi))
            high.append((dr * wr + di * wi, di * wr - dr * wi))
    return low + high


def tables(blocks, outer):
    phi = np.array(leaf_angles(blocks, math.pi / 2))
    b = np.arange(outer)
    twist = np.exp(1j * phi[:, None] * b[None, :] / outer)
    twist = np.concatenate([twist.real, twist.imag], 0).astype(np.float32)
    w = np.exp(2j * np.pi * (np.outer(b, b) % outer) / outer)
    forward = np.block([[w.real, w.imag], [-w.imag, w.real]])
    v = np.conj(w) / (blocks * outer)
    backward = np.block([[v.real, v.imag], [-v.imag, v.real]])

    def split(m):
        top = m.astype(np.float32).astype(ml_dtypes.bfloat16)
        rest = (m - top.astype(np.float64)).astype(np.float32).astype(ml_dtypes.bfloat16)
        return np.stack([top, rest])

    return twist, split(forward), split(backward)


def accurate_dot(x, m_ref):
    top = x.astype(bf16)
    rest = (x - top.astype(f32)).astype(bf16)
    dot = lambda a, b: jnp.dot(a, b, preferred_element_type=f32)
    return dot(top, m_ref[0]) + (dot(rest, m_ref[0]) + dot(top, m_ref[1]))


def send_kernel(out_gate, in_gate, values, upstream, send, held, arrived):
    blocks, width = send.shape[0], send.shape[1] // 2
    rows, channels = out_gate.shape
    part = channels // PARTS
    sources = (in_gate, values, upstream, out_gate)

    def fetch(n, p):
        at = slice(p * part, (p + 1) * part)
        return pltpu.make_async_copy(sources[n].at[:, at], held.at[n, p], arrived.at[n, p])

    for p in range(PARTS):
        for n in range(4):
            fetch(n, p).start()
    for p in range(PARTS):
        first = p * part // width
        for s in range(2):
            fetch(2 * s, p).wait()
            fetch(2 * s + 1, p).wait()
            gated = (held[2 * s, p].astype(f32) * held[2 * s + 1, p].astype(f32)).astype(bf16)
            turned = gated.T
            for n in range(part // width):
                at = slot(first + n, CTX_FIRST, blocks)
                send[at, s * width : (s + 1) * width, :] = turned[n * width : (n + 1) * width]


def forward_part(load, twist, matrix, work, width, outer):
    blocks = twist.shape[0] // 2
    for g in range(width // 16):
        coefs = [(load(i, g), None) for i in range(blocks)]
        for k, (re, im) in enumerate(evaluate(coefs, math.pi / 2)):
            cr, ci = twist[k : k + 1, :], twist[blocks + k : blocks + k + 1, :]
            at = slice(k * width + 16 * g, k * width + 16 * g + 16)
            work[at, :outer] = re * cr - im * ci
            work[at, outer:] = re * ci + im * cr
    step = 128
    for r in range(0, blocks * width, step):
        work[r : r + step, :] = accurate_dot(work[r : r + step, :], matrix)


def taps_kernel(index, taps, twist, matrix, spectrum, turned):
    blocks, outer = twist.shape[0] // 2, twist.shape[1]
    width = spectrum.shape[0] // blocks
    for i in range(blocks):
        turned[i] = taps[i * outer : (i + 1) * outer, :].astype(f32).T
    start = pl.multiple_of(index[1], 16)

    def load(i, g):
        return turned[i, pl.ds(start + 16 * g, 16), :]

    forward_part(load, twist, matrix, spectrum, width, outer)


def mix_kernel(received, taps_values, twist, forward, backward, result, work):
    blocks, width, outer = received.shape[0], received.shape[1] // 2, received.shape[2]
    for s in range(2):
        forward_part(
            lambda i, g: received[slot(i, CTX_FIRST, blocks), s * width + 16 * g : s * width + 16 * g + 16, :].astype(f32),
            twist, forward, work.at[s], width, outer,
        )
    step = 128
    for r in range(0, blocks * width, step):
        at = slice(r, r + step)
        pr, pi = work[0, at, :outer], work[0, at, outer:]
        cr, ci = work[1, at, :outer], work[1, at, outer:]
        hr, hi = taps_values[at, :outer], taps_values[at, outer:]
        filtered = jnp.concatenate([hr * pr - hi * pi, hr * pi + hi * pr], 1)
        mixed = jnp.concatenate([cr * hr + ci * hi, ci * hr - cr * hi], 1)
        lags = jnp.concatenate([cr * pr + ci * pi, ci * pr - cr * pi], 1)
        work[0, at, :] = accurate_dot(filtered, backward)
        work[1, at, :] = accurate_dot(mixed, backward)
        work[2, at, :] = accurate_dot(lags, backward)
    norm_factor = (blocks * outer) ** -0.5
    for s in range(3):
        for g in range(width // 16):
            values = []
            for k in range(blocks):
                cr, ci = twist[k : k + 1, :], twist[blocks + k : blocks + k + 1, :]
                at = slice(k * width + 16 * g, k * width + 16 * g + 16)
                re, im = work[s, at, :outer], work[s, at, outer:]
                values.append((re * cr + im * ci, im * cr - re * ci))
            for i, x in enumerate(interpolate(values, math.pi / 2, True)):
                if s == 2:
                    x = x * norm_factor
                result[slot(i, CTX_FIRST, blocks), s * width + 16 * g : s * width + 16 * g + 16, :] = x.astype(bf16)


def gather_part(back, s):
    width, blocks = back.shape[1] // 3, back.shape[0]
    parts = [back[slot(d, CTX_FIRST, blocks), s * width : (s + 1) * width, :] for d in range(blocks)]
    return jnp.concatenate(parts, 0).astype(f32).T


def lags_kernel(back, lags):
    turned = gather_part(back, 2)
    owners, rows = lags.shape[0], lags.shape[1]
    for j in range(owners):
        lags[slot(j, CH_FIRST, owners)] = turned[j * rows : (j + 1) * rows, :].astype(bf16)


def last_kernel(
    arrived, back, out_gate, in_gate, values, upstream,
    mixed_out, d_out_gate, d_in_gate, d_values, grad_filter,
):
    owners, span = arrived.shape[0], arrived.shape[2]
    for j in range(owners):
        at = slot(j, CH_FIRST, owners)
        grad_filter[:, j * span : (j + 1) * span] = arrived[at].astype(f32)
    filtered, grad_mixed = gather_part(back, 0), gather_part(back, 1)
    mixed_out[...] = (out_gate[...].astype(f32) * filtered).astype(bf16)
    d_out_gate[...] = (upstream[...].astype(f32) * filtered).astype(bf16)
    d_in_gate[...] = (grad_mixed * values[...].astype(f32)).astype(bf16)
    d_values[...] = (grad_mixed * in_gate[...].astype(f32)).astype(bf16)


def call(kernel, outs, *args, flops=1000000, vmem=VMEM, **kwargs):
    return pl.pallas_call(
        kernel,
        out_shape=outs,
        compiler_params=pltpu.CompilerParams(vmem_limit_bytes=vmem),
        cost_estimate=pl.CostEstimate(flops=flops, bytes_accessed=1 << 20, transcendentals=0),
        **kwargs,
    )(*args)


def body(out_gate, in_gate, values, filter_taps, upstream):
    rows, channels = out_gate.shape
    seq_len = filter_taps.shape[0]
    blocks = lax.axis_size("ctx")
    owners = lax.axis_size("ch")
    width = channels // blocks
    shape = jax.ShapeDtypeStruct
    twist, forward, backward = (jnp.asarray(t) for t in tables(blocks, rows))

    send = call(
        send_kernel,
        shape((blocks, 2 * width, rows), bf16),
        out_gate, in_gate, values, upstream,
        vmem=63 * 1024 * 1024 + 960 * 1024,
        in_specs=[pl.BlockSpec(memory_space=pltpu.HBM)] * 4,
        scratch_shapes=[
            pltpu.VMEM((4, PARTS, rows, channels // PARTS), bf16),
            pltpu.SemaphoreType.DMA((4, PARTS)),
        ],
    )
    received = exchange(send, "ctx", CTX_FIRST)

    me = lax.axis_index("ctx")
    first = me * width
    index = jnp.stack([first // 128, first % 128]).astype(jnp.int32)
    whole = lambda s: pl.BlockSpec(s, lambda g, index: (0,) * len(s))
    taps_values = call(
        taps_kernel,
        shape((blocks * width, 2 * rows), f32),
        index, filter_taps, twist, forward,
        grid_spec=pltpu.PrefetchScalarGridSpec(
            num_scalar_prefetch=1,
            grid=(1,),
            in_specs=[
                pl.BlockSpec((seq_len, 128), lambda g, index: (0, index[0])),
                whole(twist.shape),
                whole(forward.shape),
            ],
            out_specs=whole((blocks * width, 2 * rows)),
            scratch_shapes=[pltpu.VMEM((blocks, 128, rows), f32)],
        ),
    )
    result = call(
        mix_kernel,
        shape((blocks, 3 * width, rows), bf16),
        received, taps_values, twist, forward, backward,
        scratch_shapes=[pltpu.VMEM((3, blocks * width, 2 * rows), f32)],
    )
    back = exchange(result, "ctx", CTX_FIRST)
    lags = call(lags_kernel, shape((owners, rows // owners, channels), bf16), back)
    arrived = exchange(lags, "ch", CH_FIRST)
    out = shape((rows, channels), bf16)
    return call(
        last_kernel,
        (out,) * 4 + (shape((rows // owners, owners * channels), f32),),
        arrived, back, out_gate, in_gate, values, upstream,
    )


def solution(mesh):
    return jax.shard_map(
        body,
        mesh=mesh,
        in_specs=(P("ctx", "ch"), P("ctx", "ch"), P("ctx", "ch"), P(None, "ch"), P("ctx", "ch")),
        out_specs=(
            P("ctx", "ch"),
            P("ctx", "ch"),
            P("ctx", "ch"),
            P("ctx", "ch"),
            P(("ctx", "ch"), None),
        ),
        check_vma=False,
    )
```

```python
import math

import jax
import jax.numpy as jnp
import ml_dtypes
import numpy as np
from jax import lax
from jax.experimental import pallas as pl
from jax.experimental.pallas import tpu as pltpu
from jax.sharding import PartitionSpec as P

VMEM = 48 * 1024 * 1024
PARTS = 2
IN_FIRST, CTX_FIRST, CH_FIRST = 15, 11, 9
f32, bf16 = jnp.float32, jnp.bfloat16


def slot(i, first, count):
    return (i - first) % count


def exchange(x, axis, first):
    count = lax.axis_size(axis)
    devices = [[(first + k) % count for k in range(count)]]
    return lax.all_to_all(x, axis, 0, 0, tiled=True, axis_index_groups=devices)


def leaf_angles(count, theta):
    if count == 1:
        return [theta]
    return leaf_angles(count // 2, theta / 2) + leaf_angles(count // 2, theta / 2 + math.pi)


def evaluate(coefs, theta):
    if len(coefs) == 1:
        return coefs
    half = len(coefs) // 2
    wr, wi = math.cos(theta / 2), math.sin(theta / 2)
    plus, minus = [], []
    for (lr, li), (hr, hi) in zip(coefs[:half], coefs[half:]):
        if hi is None:
            tr, ti = hr * wr, hr * wi
            plus.append((lr + tr, ti))
            minus.append((lr - tr, -ti))
        else:
            tr, ti = hr * wr - hi * wi, hr * wi + hi * wr
            plus.append((lr + tr, li + ti))
            minus.append((lr - tr, li - ti))
    return evaluate(plus, theta / 2) + evaluate(minus, theta / 2 + math.pi)


def interpolate(values, theta, real):
    if len(values) == 1:
        return values
    half = len(values) // 2
    wr, wi = math.cos(theta / 2), math.sin(theta / 2)
    plus = interpolate(values[:half], theta / 2, False)
    minus = interpolate(values[half:], theta / 2 + math.pi, False)
    low, high = [], []
    for (pr, pi), (mr, mi) in zip(plus, minus):
        dr, di = pr - mr, pi - mi
        if real:
            low.append(pr + mr)
            high.append(dr * wr + di * wi)
        else:
            low.append((pr + mr, pi + mi))
            high.append((dr * wr + di * wi, di * wr - dr * wi))
    return low + high


def tables(blocks, outer):
    phi = np.array(leaf_angles(blocks, math.pi / 2))
    b = np.arange(outer)
    twist = np.exp(1j * phi[:, None] * b[None, :] / outer)
    twist = np.concatenate([twist.real, twist.imag], 0).astype(np.float32)
    w = np.exp(2j * np.pi * (np.outer(b, b) % outer) / outer)
    forward = np.block([[w.real, w.imag], [-w.imag, w.real]])
    v = np.conj(w) / (blocks * outer)
    backward = np.block([[v.real, v.imag], [-v.imag, v.real]])

    def split(m):
        top = m.astype(np.float32).astype(ml_dtypes.bfloat16)
        rest = (m - top.astype(np.float64)).astype(np.float32).astype(ml_dtypes.bfloat16)
        return np.stack([top, rest])

    return twist, split(forward), split(backward)


def accurate_dot(x, m_ref):
    top = x.astype(bf16)
    rest = (x - top.astype(f32)).astype(bf16)
    dot = lambda a, b: jnp.dot(a, b, preferred_element_type=f32)
    return dot(top, m_ref[0]) + (dot(rest, m_ref[0]) + dot(top, m_ref[1]))


def send_kernel(out_gate, in_gate, values, upstream, send, held, arrived):
    blocks, width = send.shape[0], send.shape[1] // 2
    rows, channels = out_gate.shape
    part = channels // PARTS
    sources = (in_gate, values, upstream, out_gate)

    def fetch(n, p):
        at = slice(p * part, (p + 1) * part)
        return pltpu.make_async_copy(sources[n].at[:, at], held.at[n, p], arrived.at[n, p])

    for p in range(PARTS):
        for n in range(4):
            fetch(n, p).start()
    for p in range(PARTS):
        first = p * part // width
        for s in range(2):
            fetch(2 * s, p).wait()
            fetch(2 * s + 1, p).wait()
            gated = (held[2 * s, p].astype(f32) * held[2 * s + 1, p].astype(f32)).astype(bf16)
            turned = gated.T
            for n in range(part // width):
                at = slot(first + n, IN_FIRST, blocks)
                send[at, s * width : (s + 1) * width, :] = turned[n * width : (n + 1) * width]


def forward_part(load, twist, matrix, work, width, outer):
    blocks = twist.shape[0] // 2
    for g in range(width // 16):
        coefs = [(load(i, g), None) for i in range(blocks)]
        for k, (re, im) in enumerate(evaluate(coefs, math.pi / 2)):
            cr, ci = twist[k : k + 1, :], twist[blocks + k : blocks + k + 1, :]
            at = slice(k * width + 16 * g, k * width + 16 * g + 16)
            work[at, :outer] = re * cr - im * ci
            work[at, outer:] = re * ci + im * cr
    step = 128
    for r in range(0, blocks * width, step):
        work[r : r + step, :] = accurate_dot(work[r : r + step, :], matrix)


def taps_kernel(index, taps, twist, matrix, spectrum, turned):
    blocks, outer = twist.shape[0] // 2, twist.shape[1]
    width = spectrum.shape[0] // blocks
    for i in range(blocks):
        turned[i] = taps[i * outer : (i + 1) * outer, :].astype(f32).T
    start = pl.multiple_of(index[1], 16)

    def load(i, g):
        return turned[i, pl.ds(start + 16 * g, 16), :]

    forward_part(load, twist, matrix, spectrum, width, outer)


def mix_kernel(received, taps_values, twist, forward, backward, result, work):
    blocks, width, outer = received.shape[0], received.shape[1] // 2, received.shape[2]
    for s in range(2):
        forward_part(
            lambda i, g: received[slot(i, IN_FIRST, blocks), s * width + 16 * g : s * width + 16 * g + 16, :].astype(f32),
            twist, forward, work.at[s], width, outer,
        )
    step = 128
    for r in range(0, blocks * width, step):
        at = slice(r, r + step)
        pr, pi = work[0, at, :outer], work[0, at, outer:]
        cr, ci = work[1, at, :outer], work[1, at, outer:]
        hr, hi = taps_values[at, :outer], taps_values[at, outer:]
        filtered = jnp.concatenate([hr * pr - hi * pi, hr * pi + hi * pr], 1)
        mixed = jnp.concatenate([cr * hr + ci * hi, ci * hr - cr * hi], 1)
        lags = jnp.concatenate([cr * pr + ci * pi, ci * pr - cr * pi], 1)
        work[0, at, :] = accurate_dot(filtered, backward)
        work[1, at, :] = accurate_dot(mixed, backward)
        work[2, at, :] = accurate_dot(lags, backward)
    norm_factor = (blocks * outer) ** -0.5
    for s in range(3):
        for g in range(width // 16):
            values = []
            for k in range(blocks):
                cr, ci = twist[k : k + 1, :], twist[blocks + k : blocks + k + 1, :]
                at = slice(k * width + 16 * g, k * width + 16 * g + 16)
                re, im = work[s, at, :outer], work[s, at, outer:]
                values.append((re * cr + im * ci, im * cr - re * ci))
            for i, x in enumerate(interpolate(values, math.pi / 2, True)):
                if s == 2:
                    x = x * norm_factor
                result[slot(i, CTX_FIRST, blocks), s * width + 16 * g : s * width + 16 * g + 16, :] = x.astype(bf16)


def gather_part(back, s):
    width, blocks = back.shape[1] // 3, back.shape[0]
    parts = [back[slot(d, CTX_FIRST, blocks), s * width : (s + 1) * width, :] for d in range(blocks)]
    return jnp.concatenate(parts, 0).astype(f32).T


def lags_kernel(back, lags):
    turned = gather_part(back, 2)
    owners, rows = lags.shape[0], lags.shape[1]
    for j in range(owners):
        lags[slot(j, CH_FIRST, owners)] = turned[j * rows : (j + 1) * rows, :].astype(bf16)


def last_kernel(
    arrived, back, out_gate, in_gate, values, upstream,
    mixed_out, d_out_gate, d_in_gate, d_values, grad_filter,
):
    owners, span = arrived.shape[0], arrived.shape[2]
    for j in range(owners):
        at = slot(j, CH_FIRST, owners)
        grad_filter[:, j * span : (j + 1) * span] = arrived[at].astype(f32)
    filtered, grad_mixed = gather_part(back, 0), gather_part(back, 1)
    mixed_out[...] = (out_gate[...].astype(f32) * filtered).astype(bf16)
    d_out_gate[...] = (upstream[...].astype(f32) * filtered).astype(bf16)
    d_in_gate[...] = (grad_mixed * values[...].astype(f32)).astype(bf16)
    d_values[...] = (grad_mixed * in_gate[...].astype(f32)).astype(bf16)


def call(kernel, outs, *args, flops=1000000, vmem=VMEM, **kwargs):
    return pl.pallas_call(
        kernel,
        out_shape=outs,
        compiler_params=pltpu.CompilerParams(vmem_limit_bytes=vmem),
        cost_estimate=pl.CostEstimate(flops=flops, bytes_accessed=1 << 20, transcendentals=0),
        **kwargs,
    )(*args)


def body(out_gate, in_gate, values, filter_taps, upstream):
    rows, channels = out_gate.shape
    seq_len = filter_taps.shape[0]
    blocks = lax.axis_size("ctx")
    owners = lax.axis_size("ch")
    width = channels // blocks
    shape = jax.ShapeDtypeStruct
    twist, forward, backward = (jnp.asarray(t) for t in tables(blocks, rows))

    send = call(
        send_kernel,
        shape((blocks, 2 * width, rows), bf16),
        out_gate, in_gate, values, upstream,
        vmem=63 * 1024 * 1024 + 960 * 1024,
        in_specs=[pl.BlockSpec(memory_space=pltpu.HBM)] * 4,
        scratch_shapes=[
            pltpu.VMEM((4, PARTS, rows, channels // PARTS), bf16),
            pltpu.SemaphoreType.DMA((4, PARTS)),
        ],
    )
    received = exchange(send, "ctx", IN_FIRST)

    me = lax.axis_index("ctx")
    first = me * width
    index = jnp.stack([first // 128, first % 128]).astype(jnp.int32)
    whole = lambda s: pl.BlockSpec(s, lambda g, index: (0,) * len(s))
    taps_values = call(
        taps_kernel,
        shape((blocks * width, 2 * rows), f32),
        index, filter_taps, twist, forward,
        grid_spec=pltpu.PrefetchScalarGridSpec(
            num_scalar_prefetch=1,
            grid=(1,),
            in_specs=[
                pl.BlockSpec((seq_len, 128), lambda g, index: (0, index[0])),
                whole(twist.shape),
                whole(forward.shape),
            ],
            out_specs=whole((blocks * width, 2 * rows)),
            scratch_shapes=[pltpu.VMEM((blocks, 128, rows), f32)],
        ),
    )
    result = call(
        mix_kernel,
        shape((blocks, 3 * width, rows), bf16),
        received, taps_values, twist, forward, backward,
        scratch_shapes=[pltpu.VMEM((3, blocks * width, 2 * rows), f32)],
    )
    back = exchange(result, "ctx", CTX_FIRST)
    lags = call(lags_kernel, shape((owners, rows // owners, channels), bf16), back)
    arrived = exchange(lags, "ch", CH_FIRST)
    out = shape((rows, channels), bf16)
    return call(
        last_kernel,
        (out,) * 4 + (shape((rows // owners, owners * channels), f32),),
        arrived, back, out_gate, in_gate, values, upstream,
    )


def solution(mesh):
    return jax.shard_map(
        body,
        mesh=mesh,
        in_specs=(P("ctx", "ch"), P("ctx", "ch"), P("ctx", "ch"), P(None, "ch"), P("ctx", "ch")),
        out_specs=(
            P("ctx", "ch"),
            P("ctx", "ch"),
            P("ctx", "ch"),
            P("ctx", "ch"),
            P(("ctx", "ch"), None),
        ),
        check_vma=False,
    )
```

```python
import math

import jax
import jax.numpy as jnp
import ml_dtypes
import numpy as np
from jax import lax
from jax.experimental import pallas as pl
from jax.experimental.pallas import tpu as pltpu
from jax.sharding import PartitionSpec as P

VMEM = 48 * 1024 * 1024
PARTS = 2
IN_FIRST, CTX_FIRST, CH_FIRST = 15, 11, 9
f32, bf16 = jnp.float32, jnp.bfloat16


def slot(i, first, count):
    return (i - first) % count


def exchange(x, axis, first):
    count = lax.axis_size(axis)
    devices = [[(first + k) % count for k in range(count)]]
    return lax.all_to_all(x, axis, 0, 0, tiled=True, axis_index_groups=devices)


def leaf_angles(count, theta):
    if count == 1:
        return [theta]
    return leaf_angles(count // 2, theta / 2) + leaf_angles(count // 2, theta / 2 + math.pi)


def evaluate(coefs, theta):
    if len(coefs) == 1:
        return coefs
    half = len(coefs) // 2
    wr, wi = math.cos(theta / 2), math.sin(theta / 2)
    plus, minus = [], []
    for (lr, li), (hr, hi) in zip(coefs[:half], coefs[half:]):
        if hi is None:
            tr, ti = hr * wr, hr * wi
            plus.append((lr + tr, ti))
            minus.append((lr - tr, -ti))
        else:
            tr, ti = hr * wr - hi * wi, hr * wi + hi * wr
            plus.append((lr + tr, li + ti))
            minus.append((lr - tr, li - ti))
    return evaluate(plus, theta / 2) + evaluate(minus, theta / 2 + math.pi)


def interpolate(values, theta, real):
    if len(values) == 1:
        return values
    half = len(values) // 2
    wr, wi = math.cos(theta / 2), math.sin(theta / 2)
    plus = interpolate(values[:half], theta / 2, False)
    minus = interpolate(values[half:], theta / 2 + math.pi, False)
    low, high = [], []
    for (pr, pi), (mr, mi) in zip(plus, minus):
        dr, di = pr - mr, pi - mi
        if real:
            low.append(pr + mr)
            high.append(dr * wr + di * wi)
        else:
            low.append((pr + mr, pi + mi))
            high.append((dr * wr + di * wi, di * wr - dr * wi))
    return low + high


def tables(blocks, outer):
    phi = np.array(leaf_angles(blocks, math.pi / 2))
    b = np.arange(outer)
    twist = np.exp(1j * phi[:, None] * b[None, :] / outer)
    twist = np.concatenate([twist.real, twist.imag], 0).astype(np.float32)
    w = np.exp(2j * np.pi * (np.outer(b, b) % outer) / outer)
    forward = np.block([[w.real, w.imag], [-w.imag, w.real]])
    v = np.conj(w) / (blocks * outer)
    backward = np.block([[v.real, v.imag], [-v.imag, v.real]])

    def split(m):
        top = m.astype(np.float32).astype(ml_dtypes.bfloat16)
        rest = (m - top.astype(np.float64)).astype(np.float32).astype(ml_dtypes.bfloat16)
        return np.stack([top, rest])

    rest, parts = np.concatenate([twist[:blocks], twist[blocks:]], 1), []
    for _ in range(3):
        parts.append(rest.astype(ml_dtypes.bfloat16))
        rest = rest - parts[-1].astype(np.float32)
    table = np.concatenate([*split(forward), *parts], 0)
    return twist, split(forward), split(backward), table


def read_table(table, twist):
    blocks, outer = twist.shape[0] // 2, twist.shape[1]
    rest = table[4 * outer :, :].astype(f32)
    total = (rest[2 * blocks :] + rest[blocks : 2 * blocks]) + rest[:blocks]
    twist[:blocks, :] = total[:, :outer]
    twist[blocks:, :] = total[:, outer:]
    return table.at[: 2 * outer], table.at[2 * outer : 4 * outer]


def accurate_dot(x, m_ref):
    top = x.astype(bf16)
    rest = (x - top.astype(f32)).astype(bf16)
    dot = lambda a, b: jnp.dot(a, b, preferred_element_type=f32)
    return dot(top, m_ref[0][...]) + (dot(rest, m_ref[0][...]) + dot(top, m_ref[1][...]))


def send_kernel(out_gate, in_gate, values, upstream, send, held, arrived):
    blocks, width = send.shape[0], send.shape[1] // 2
    rows, channels = out_gate.shape
    part = channels // PARTS
    sources = (in_gate, values, upstream, out_gate)

    def fetch(n, p):
        at = slice(p * part, (p + 1) * part)
        return pltpu.make_async_copy(sources[n].at[:, at], held.at[n, p], arrived.at[n, p])

    for p in range(PARTS):
        for n in range(4):
            fetch(n, p).start()
    for p in range(PARTS):
        first = p * part // width
        for s in range(2):
            fetch(2 * s, p).wait()
            fetch(2 * s + 1, p).wait()
            gated = (held[2 * s, p].astype(f32) * held[2 * s + 1, p].astype(f32)).astype(bf16)
            turned = gated.T
            for n in range(part // width):
                at = slot(first + n, IN_FIRST, blocks)
                send[at, s * width : (s + 1) * width, :] = turned[n * width : (n + 1) * width]


def forward_part(load, twist, matrix, work, width, outer):
    blocks = twist.shape[0] // 2
    for g in range(width // 16):
        coefs = [(load(i, g), None) for i in range(blocks)]
        for k, (re, im) in enumerate(evaluate(coefs, math.pi / 2)):
            cr, ci = twist[k : k + 1, :], twist[blocks + k : blocks + k + 1, :]
            at = slice(k * width + 16 * g, k * width + 16 * g + 16)
            work[at, :outer] = re * cr - im * ci
            work[at, outer:] = re * ci + im * cr
    step = 128
    for r in range(0, blocks * width, step):
        work[r : r + step, :] = accurate_dot(work[r : r + step, :], matrix)


def taps_kernel(index, taps, table, spectrum, turned, twist):
    matrix = read_table(table, twist)
    blocks, outer = twist.shape[0] // 2, twist.shape[1]
    width = spectrum.shape[0] // blocks
    for i in range(blocks):
        turned[i] = taps[i * outer : (i + 1) * outer, :].astype(f32).T
    start = pl.multiple_of(index[1], 16)

    def load(i, g):
        return turned[i, pl.ds(start + 16 * g, 16), :]

    forward_part(load, twist, matrix, spectrum, width, outer)


def mix_kernel(received, taps_values, twist, forward, backward, result, work):
    blocks, width, outer = received.shape[0], received.shape[1] // 2, received.shape[2]
    for s in range(2):
        forward_part(
            lambda i, g: received[slot(i, IN_FIRST, blocks), s * width + 16 * g : s * width + 16 * g + 16, :].astype(f32),
            twist, forward, work.at[s], width, outer,
        )
    step = 128
    for r in range(0, blocks * width, step):
        at = slice(r, r + step)
        pr, pi = work[0, at, :outer], work[0, at, outer:]
        cr, ci = work[1, at, :outer], work[1, at, outer:]
        hr, hi = taps_values[at, :outer], taps_values[at, outer:]
        filtered = jnp.concatenate([hr * pr - hi * pi, hr * pi + hi * pr], 1)
        mixed = jnp.concatenate([cr * hr + ci * hi, ci * hr - cr * hi], 1)
        lags = jnp.concatenate([cr * pr + ci * pi, ci * pr - cr * pi], 1)
        work[0, at, :] = accurate_dot(filtered, backward)
        work[1, at, :] = accurate_dot(mixed, backward)
        work[2, at, :] = accurate_dot(lags, backward)
    norm_factor = (blocks * outer) ** -0.5
    for s in range(3):
        for g in range(width // 16):
            values = []
            for k in range(blocks):
                cr, ci = twist[k : k + 1, :], twist[blocks + k : blocks + k + 1, :]
                at = slice(k * width + 16 * g, k * width + 16 * g + 16)
                re, im = work[s, at, :outer], work[s, at, outer:]
                values.append((re * cr + im * ci, im * cr - re * ci))
            for i, x in enumerate(interpolate(values, math.pi / 2, True)):
                if s == 2:
                    x = x * norm_factor
                result[slot(i, CTX_FIRST, blocks), s * width + 16 * g : s * width + 16 * g + 16, :] = x.astype(bf16)


def gather_part(back, s):
    width, blocks = back.shape[1] // 3, back.shape[0]
    parts = [back[slot(d, CTX_FIRST, blocks), s * width : (s + 1) * width, :] for d in range(blocks)]
    return jnp.concatenate(parts, 0).astype(f32).T


def lags_kernel(back, lags):
    turned = gather_part(back, 2)
    owners, rows = lags.shape[0], lags.shape[1]
    for j in range(owners):
        lags[slot(j, CH_FIRST, owners)] = turned[j * rows : (j + 1) * rows, :].astype(bf16)


def last_kernel(
    arrived, back, out_gate, in_gate, values, upstream,
    mixed_out, d_out_gate, d_in_gate, d_values, grad_filter,
):
    owners, span = arrived.shape[0], arrived.shape[2]
    for j in range(owners):
        at = slot(j, CH_FIRST, owners)
        grad_filter[:, j * span : (j + 1) * span] = arrived[at].astype(f32)
    filtered, grad_mixed = gather_part(back, 0), gather_part(back, 1)
    mixed_out[...] = (out_gate[...].astype(f32) * filtered).astype(bf16)
    d_out_gate[...] = (upstream[...].astype(f32) * filtered).astype(bf16)
    d_in_gate[...] = (grad_mixed * values[...].astype(f32)).astype(bf16)
    d_values[...] = (grad_mixed * in_gate[...].astype(f32)).astype(bf16)


def call(kernel, outs, *args, flops=1000000, vmem=VMEM, **kwargs):
    return pl.pallas_call(
        kernel,
        out_shape=outs,
        compiler_params=pltpu.CompilerParams(vmem_limit_bytes=vmem),
        cost_estimate=pl.CostEstimate(flops=flops, bytes_accessed=1 << 20, transcendentals=0),
        **kwargs,
    )(*args)


def body(out_gate, in_gate, values, filter_taps, upstream):
    rows, channels = out_gate.shape
    seq_len = filter_taps.shape[0]
    blocks = lax.axis_size("ctx")
    owners = lax.axis_size("ch")
    width = channels // blocks
    shape = jax.ShapeDtypeStruct
    twist, forward, backward, table = (jnp.asarray(t) for t in tables(blocks, rows))

    send = call(
        send_kernel,
        shape((blocks, 2 * width, rows), bf16),
        out_gate, in_gate, values, upstream,
        vmem=63 * 1024 * 1024 + 960 * 1024,
        in_specs=[pl.BlockSpec(memory_space=pltpu.HBM)] * 4,
        scratch_shapes=[
            pltpu.VMEM((4, PARTS, rows, channels // PARTS), bf16),
            pltpu.SemaphoreType.DMA((4, PARTS)),
        ],
    )
    received = exchange(send, "ctx", IN_FIRST)

    me = lax.axis_index("ctx")
    first = me * width
    index = jnp.stack([first // 128, first % 128]).astype(jnp.int32)
    whole = lambda s: pl.BlockSpec(s, lambda g, index: (0,) * len(s))
    taps_values = call(
        taps_kernel,
        shape((blocks * width, 2 * rows), f32),
        index, filter_taps, table,
        grid_spec=pltpu.PrefetchScalarGridSpec(
            num_scalar_prefetch=1,
            grid=(1,),
            in_specs=[
                pl.BlockSpec((seq_len, 128), lambda g, index: (0, index[0])),
                whole(table.shape),
            ],
            out_specs=whole((blocks * width, 2 * rows)),
            scratch_shapes=[
                pltpu.VMEM((blocks, 128, rows), f32),
                pltpu.VMEM((2 * blocks, rows), f32),
            ],
        ),
    )
    result = call(
        mix_kernel,
        shape((blocks, 3 * width, rows), bf16),
        received, taps_values, twist, forward, backward,
        scratch_shapes=[pltpu.VMEM((3, blocks * width, 2 * rows), f32)],
    )
    back = exchange(result, "ctx", CTX_FIRST)
    lags = call(lags_kernel, shape((owners, rows // owners, channels), bf16), back)
    arrived = exchange(lags, "ch", CH_FIRST)
    out = shape((rows, channels), bf16)
    return call(
        last_kernel,
        (out,) * 4 + (shape((rows // owners, owners * channels), f32),),
        arrived, back, out_gate, in_gate, values, upstream,
    )


def solution(mesh):
    return jax.shard_map(
        body,
        mesh=mesh,
        in_specs=(P("ctx", "ch"), P("ctx", "ch"), P("ctx", "ch"), P(None, "ch"), P("ctx", "ch")),
        out_specs=(
            P("ctx", "ch"),
            P("ctx", "ch"),
            P("ctx", "ch"),
            P("ctx", "ch"),
            P(("ctx", "ch"), None),
        ),
        check_vma=False,
    )
```

```python
import math

import jax
import jax.numpy as jnp
import ml_dtypes
import numpy as np
from jax import lax
from jax.experimental import pallas as pl
from jax.experimental.pallas import tpu as pltpu
from jax.sharding import PartitionSpec as P

VMEM = 48 * 1024 * 1024
PARTS = 2
IN_FIRST, CTX_FIRST, CH_FIRST = 15, 11, 11
f32, bf16 = jnp.float32, jnp.bfloat16


def slot(i, first, count):
    return (i - first) % count


def exchange(x, axis, first):
    count = lax.axis_size(axis)
    devices = [[(first + k) % count for k in range(count)]]
    return lax.all_to_all(x, axis, 0, 0, tiled=True, axis_index_groups=devices)


def leaf_angles(count, theta):
    if count == 1:
        return [theta]
    return leaf_angles(count // 2, theta / 2) + leaf_angles(count // 2, theta / 2 + math.pi)


def evaluate(coefs, theta):
    if len(coefs) == 1:
        return coefs
    half = len(coefs) // 2
    wr, wi = math.cos(theta / 2), math.sin(theta / 2)
    plus, minus = [], []
    for (lr, li), (hr, hi) in zip(coefs[:half], coefs[half:]):
        if hi is None:
            tr, ti = hr * wr, hr * wi
            plus.append((lr + tr, ti))
            minus.append((lr - tr, -ti))
        else:
            tr, ti = hr * wr - hi * wi, hr * wi + hi * wr
            plus.append((lr + tr, li + ti))
            minus.append((lr - tr, li - ti))
    return evaluate(plus, theta / 2) + evaluate(minus, theta / 2 + math.pi)


def interpolate(values, theta, real):
    if len(values) == 1:
        return values
    half = len(values) // 2
    wr, wi = math.cos(theta / 2), math.sin(theta / 2)
    plus = interpolate(values[:half], theta / 2, False)
    minus = interpolate(values[half:], theta / 2 + math.pi, False)
    low, high = [], []
    for (pr, pi), (mr, mi) in zip(plus, minus):
        dr, di = pr - mr, pi - mi
        if real:
            low.append(pr + mr)
            high.append(dr * wr + di * wi)
        else:
            low.append((pr + mr, pi + mi))
            high.append((dr * wr + di * wi, di * wr - dr * wi))
    return low + high


def tables(blocks, outer):
    phi = np.array(leaf_angles(blocks, math.pi / 2))
    b = np.arange(outer)
    twist = np.exp(1j * phi[:, None] * b[None, :] / outer)
    twist = np.concatenate([twist.real, twist.imag], 0).astype(np.float32)
    w = np.exp(2j * np.pi * (np.outer(b, b) % outer) / outer)
    forward = np.block([[w.real, w.imag], [-w.imag, w.real]])
    v = np.conj(w) / (blocks * outer)
    backward = np.block([[v.real, v.imag], [-v.imag, v.real]])

    def split(m):
        top = m.astype(np.float32).astype(ml_dtypes.bfloat16)
        rest = (m - top.astype(np.float64)).astype(np.float32).astype(ml_dtypes.bfloat16)
        return np.stack([top, rest])

    return twist, split(forward), split(backward)


def accurate_dot(x, m_ref):
    top = x.astype(bf16)
    rest = (x - top.astype(f32)).astype(bf16)
    dot = lambda a, b: jnp.dot(a, b, preferred_element_type=f32)
    return dot(top, m_ref[0]) + (dot(rest, m_ref[0]) + dot(top, m_ref[1]))


def send_kernel(out_gate, in_gate, values, upstream, send, held, arrived):
    blocks, width = send.shape[0], send.shape[1] // 2
    rows, channels = out_gate.shape
    part = channels // PARTS
    sources = (in_gate, values, upstream, out_gate)

    def fetch(n, p):
        at = slice(p * part, (p + 1) * part)
        return pltpu.make_async_copy(sources[n].at[:, at], held.at[n, p], arrived.at[n, p])

    for p in range(PARTS):
        for n in range(4):
            fetch(n, p).start()
    for p in range(PARTS):
        first = p * part // width
        for s in range(2):
            fetch(2 * s, p).wait()
            fetch(2 * s + 1, p).wait()
            gated = (held[2 * s, p].astype(f32) * held[2 * s + 1, p].astype(f32)).astype(bf16)
            turned = gated.T
            for n in range(part // width):
                at = slot(first + n, IN_FIRST, blocks)
                send[at, s * width : (s + 1) * width, :] = turned[n * width : (n + 1) * width]


def forward_part(load, twist, matrix, work, width, outer):
    blocks = twist.shape[0] // 2
    for g in range(width // 16):
        coefs = [(load(i, g), None) for i in range(blocks)]
        for k, (re, im) in enumerate(evaluate(coefs, math.pi / 2)):
            cr, ci = twist[k : k + 1, :], twist[blocks + k : blocks + k + 1, :]
            at = slice(k * width + 16 * g, k * width + 16 * g + 16)
            work[at, :outer] = re * cr - im * ci
            work[at, outer:] = re * ci + im * cr
    step = 128
    for r in range(0, blocks * width, step):
        work[r : r + step, :] = accurate_dot(work[r : r + step, :], matrix)


def taps_kernel(index, taps, twist, matrix, spectrum, turned):
    blocks, outer = twist.shape[0] // 2, twist.shape[1]
    width = spectrum.shape[0] // blocks
    for i in range(blocks):
        turned[i] = taps[i * outer : (i + 1) * outer, :].astype(f32).T
    start = pl.multiple_of(index[1], 16)

    def load(i, g):
        return turned[i, pl.ds(start + 16 * g, 16), :]

    forward_part(load, twist, matrix, spectrum, width, outer)


def mix_kernel(received, taps_values, twist, forward, backward, result, work):
    blocks, width, outer = received.shape[0], received.shape[1] // 2, received.shape[2]
    for s in range(2):
        forward_part(
            lambda i, g: received[slot(i, IN_FIRST, blocks), s * width + 16 * g : s * width + 16 * g + 16, :].astype(f32),
            twist, forward, work.at[s], width, outer,
        )
    step = 128
    for r in range(0, blocks * width, step):
        at = slice(r, r + step)
        pr, pi = work[0, at, :outer], work[0, at, outer:]
        cr, ci = work[1, at, :outer], work[1, at, outer:]
        hr, hi = taps_values[at, :outer], taps_values[at, outer:]
        filtered = jnp.concatenate([hr * pr - hi * pi, hr * pi + hi * pr], 1)
        mixed = jnp.concatenate([cr * hr + ci * hi, ci * hr - cr * hi], 1)
        lags = jnp.concatenate([cr * pr + ci * pi, ci * pr - cr * pi], 1)
        work[0, at, :] = accurate_dot(filtered, backward)
        work[1, at, :] = accurate_dot(mixed, backward)
        work[2, at, :] = accurate_dot(lags, backward)
    norm_factor = (blocks * outer) ** -0.5
    for s in range(3):
        for g in range(width // 16):
            values = []
            for k in range(blocks):
                cr, ci = twist[k : k + 1, :], twist[blocks + k : blocks + k + 1, :]
                at = slice(k * width + 16 * g, k * width + 16 * g + 16)
                re, im = work[s, at, :outer], work[s, at, outer:]
                values.append((re * cr + im * ci, im * cr - re * ci))
            for i, x in enumerate(interpolate(values, math.pi / 2, True)):
                if s == 2:
                    x = x * norm_factor
                result[slot(i, CTX_FIRST, blocks), s * width + 16 * g : s * width + 16 * g + 16, :] = x.astype(bf16)


def gather_part(back, s):
    width, blocks = back.shape[1] // 3, back.shape[0]
    parts = [back[slot(d, CTX_FIRST, blocks), s * width : (s + 1) * width, :] for d in range(blocks)]
    return jnp.concatenate(parts, 0).astype(f32).T


def lags_kernel(back, lags):
    turned = gather_part(back, 2)
    owners, rows = lags.shape[0], lags.shape[1]
    for j in range(owners):
        lags[slot(j, CH_FIRST, owners)] = turned[j * rows : (j + 1) * rows, :].astype(bf16)


def last_kernel(
    arrived, back, out_gate, in_gate, values, upstream,
    mixed_out, d_out_gate, d_in_gate, d_values, grad_filter,
):
    owners, span = arrived.shape[0], arrived.shape[2]
    for j in range(owners):
        at = slot(j, CH_FIRST, owners)
        grad_filter[:, j * span : (j + 1) * span] = arrived[at].astype(f32)
    filtered, grad_mixed = gather_part(back, 0), gather_part(back, 1)
    mixed_out[...] = (out_gate[...].astype(f32) * filtered).astype(bf16)
    d_out_gate[...] = (upstream[...].astype(f32) * filtered).astype(bf16)
    d_in_gate[...] = (grad_mixed * values[...].astype(f32)).astype(bf16)
    d_values[...] = (grad_mixed * in_gate[...].astype(f32)).astype(bf16)


def call(kernel, outs, *args, flops=1000000, vmem=VMEM, **kwargs):
    return pl.pallas_call(
        kernel,
        out_shape=outs,
        compiler_params=pltpu.CompilerParams(vmem_limit_bytes=vmem),
        cost_estimate=pl.CostEstimate(flops=flops, bytes_accessed=1 << 20, transcendentals=0),
        **kwargs,
    )(*args)


def body(out_gate, in_gate, values, filter_taps, upstream):
    rows, channels = out_gate.shape
    seq_len = filter_taps.shape[0]
    blocks = lax.axis_size("ctx")
    owners = lax.axis_size("ch")
    width = channels // blocks
    shape = jax.ShapeDtypeStruct
    twist, forward, backward = (jnp.asarray(t) for t in tables(blocks, rows))

    send = call(
        send_kernel,
        shape((blocks, 2 * width, rows), bf16),
        out_gate, in_gate, values, upstream,
        vmem=63 * 1024 * 1024 + 960 * 1024,
        in_specs=[pl.BlockSpec(memory_space=pltpu.HBM)] * 4,
        scratch_shapes=[
            pltpu.VMEM((4, PARTS, rows, channels // PARTS), bf16),
            pltpu.SemaphoreType.DMA((4, PARTS)),
        ],
    )
    received = exchange(send, "ctx", IN_FIRST)

    me = lax.axis_index("ctx")
    first = me * width
    index = jnp.stack([first // 128, first % 128]).astype(jnp.int32)
    whole = lambda s: pl.BlockSpec(s, lambda g, index: (0,) * len(s))
    taps_values = call(
        taps_kernel,
        shape((blocks * width, 2 * rows), f32),
        index, filter_taps, twist, forward,
        grid_spec=pltpu.PrefetchScalarGridSpec(
            num_scalar_prefetch=1,
            grid=(1,),
            in_specs=[
                pl.BlockSpec((seq_len, 128), lambda g, index: (0, index[0])),
                whole(twist.shape),
                whole(forward.shape),
            ],
            out_specs=whole((blocks * width, 2 * rows)),
            scratch_shapes=[pltpu.VMEM((blocks, 128, rows), f32)],
        ),
    )
    result = call(
        mix_kernel,
        shape((blocks, 3 * width, rows), bf16),
        received, taps_values, twist, forward, backward,
        scratch_shapes=[pltpu.VMEM((3, blocks * width, 2 * rows), f32)],
    )
    back = exchange(result, "ctx", CTX_FIRST)
    lags = call(lags_kernel, shape((owners, rows // owners, channels), bf16), back)
    arrived = exchange(lags, "ch", CH_FIRST)
    out = shape((rows, channels), bf16)
    return call(
        last_kernel,
        (out,) * 4 + (shape((rows // owners, owners * channels), f32),),
        arrived, back, out_gate, in_gate, values, upstream,
    )


def solution(mesh):
    return jax.shard_map(
        body,
        mesh=mesh,
        in_specs=(P("ctx", "ch"), P("ctx", "ch"), P("ctx", "ch"), P(None, "ch"), P("ctx", "ch")),
        out_specs=(
            P("ctx", "ch"),
            P("ctx", "ch"),
            P("ctx", "ch"),
            P("ctx", "ch"),
            P(("ctx", "ch"), None),
        ),
        check_vma=False,
    )
```
